32 devices in a mesh: dp: 4 (over z), expert: 8 (over y, x, core).
Axes of the slice: x: 2, y: 2, z: 4, core: 2. Of those that a mesh axis runs over, the one named last changes fastest.
Arguments:
- tokens: bfloat16 [4096, 1280], P(('dp', 'expert')), may hold values from -6 to 6
- cotangent: bfloat16 [4096, 1280], P(('dp', 'expert')), may hold values from -6 to 6
- routes: int32 [4096, 7], P(('dp', 'expert')), may hold values from 0 to 31, all different within a row; in each aligned block of 128 rows (0 to 127, 128 to 255, ...) at most 48 rows name the same one
- doc_ids: int32 [32, 128], P(('dp', 'expert')), may hold values from 0 to 3, never falling along the last dimension, each value on 1 to 64 neighbouring positions
- attn_weight: float32 [4, 1280, 1280], P(None, ('dp', 'expert')), may hold values from -0.15625 to 0.15625
- attn_momentum: float32 [4, 1280, 1280], P(None, ('dp', 'expert')), may hold values from -384 to 384
- attn_average: float32 [4, 1280, 1280], P(None, ('dp', 'expert')), may hold values from -0.15625 to 0.15625
- shared_weight: float32 [3, 1280, 896], P(None, ('dp', 'expert')), may hold values from -0.15625 to 0.15625
- shared_momentum: float32 [3, 1280, 896], P(None, ('dp', 'expert')), may hold values from -192 to 192
- shared_average: float32 [3, 1280, 896], P(None, ('dp', 'expert')), may hold values from -0.15625 to 0.15625
- router_weight: float32 [1280, 32], P(('dp', 'expert')), may hold values from -0.078125 to 0.078125
- router_momentum: float32 [1280, 32], P(('dp', 'expert')), may hold values from -512 to 512
- router_average: float32 [1280, 32], P(('dp', 'expert')), may hold values from -0.078125 to 0.078125
- gain_weight: float32 [2, 1280], P(None, ('dp', 'expert')), may hold values from 0.5 to 1.5
- gain_momentum: float32 [2, 1280], P(None, ('dp', 'expert')), may hold values from -384 to 384
- gain_average: float32 [2, 1280], P(None, ('dp', 'expert')), may hold values from 0.1 to 1.9
- expert_weight: float32 [32, 3, 1280, 896], P('expert', None, 'dp'), may hold values from -0.15625 to 0.15625
- expert_momentum: float32 [32, 3, 1280, 896], P('expert', None, 'dp'), may hold values from -16 to 16
- expert_average: float32 [32, 3, 1280, 896], P('expert', None, 'dp'), may hold values from -0.15625 to 0.15625
Outputs:
- layer_out: bfloat16 [4096, 1280], P(('dp', 'expert'))
- input_grad: float32 [4096, 1280], P(('dp', 'expert'))
- attn_new: float32 [4, 1280, 1280], P(None, ('dp', 'expert'))
- attn_moment: float32 [4, 1280, 1280], P(None, ('dp', 'expert'))
- attn_mean: float32 [4, 1280, 1280], P(None, ('dp', 'expert'))
- shared_new: float32 [3, 1280, 896], P(None, ('dp', 'expert'))
- shared_moment: float32 [3, 1280, 896], P(None, ('dp', 'expert'))
- shared_mean: float32 [3, 1280, 896], P(None, ('dp', 'expert'))
- router_new: float32 [1280, 32], P(('dp', 'expert'))
- router_moment: float32 [1280, 32], P(('dp', 'expert'))
- router_mean: float32 [1280, 32], P(('dp', 'expert'))
- gain_new: float32 [2, 1280], P(None, ('dp', 'expert'))
- gain_moment: float32 [2, 1280], P(None, ('dp', 'expert'))
- gain_mean: float32 [2, 1280], P(None, ('dp', 'expert'))
- expert_new: float32 [32, 3, 1280, 896], P('expert', None, 'dp')
- expert_moment: float32 [32, 3, 1280, 896], P('expert', None, 'dp')
- expert_mean: float32 [32, 3, 1280, 896], P('expert', None, 'dp')
- sublayer_rms: float32 [32, 2], P(('dp', 'expert'))
The draws below stay inside these ranges and needn't reach their ends.
Inputs may be any that keep to these rules, and one draw needn't show every extreme that they name: `routes`: each row names 7 different experts; in each aligned block of 128 rows (one sequence) no expert is named more than 48 times, a bound that some block reaches. `doc_ids`: never falls along a sequence; each of the 4 documents holds 1 to 64 positions.
All inputs are finite; a program needn't handle non-finite values.
Results may differ from the reference program's by a relative error of at most 0.012.
Values may be sent and summed in bfloat16 or wider, within the bound.
No kernel may reach another device: no remote copies, remote signals or barrier semaphores. Data moves between devices by JAX's collectives and lax.ppermute only.
A program may use at most 384 MiB of HBM per device.

```python
import math
import jax
import jax.numpy as jnp
import numpy as np
from jax import lax

D = 1280
HEADS = 10
HD = 128
FF = 896
TOPK = 7
TOK_DEV = 128
DOCS = 4
STEP = 3
SEQS = 32
TOKENS = 4096
EXPERTS = 32
CAP = 48
EXPERT_ROWS = 896


def level_of(rng, shape, pieces, least, top_value):
    def one(dim, parts):
        heights = jax.random.uniform(jax.random.fold_in(jax.random.fold_in(rng, 6), dim), (parts,), jnp.float32, least / len(pieces), top_value / len(pieces))
        return jnp.repeat(jnp.exp(heights), shape[dim] // parts).reshape((-1,) + (1,) * (len(shape) - dim - 1))

    level = one(*pieces[0])
    for cut in pieces[1:]:
        level = level * one(*cut)
    return level


def profile(count, total, limit, slope):
    loads = [(1 << 20) // math.isqrt(standing ** slope) + 1 for standing in range(2, count + 1)]
    spare, given = total - limit - (count - 1), [1] * (count - 1)
    while spare > 0:
        movable = [i for i in range(count - 1) if given[i] < limit]
        pool, budget = sum([loads[i] for i in movable]), spare
        for i in movable:
            addition = min(limit - given[i], max(1, budget * loads[i] // pool), spare)
            given[i] = given[i] + addition
            spare = spare - addition
    return np.array([limit] + given)


def ragged(rng, amount, total, most, lean):
    if amount == 2:
        one = jax.random.randint(rng, (), max(1, total - most), min(most, total - 1) + 1)
        return jnp.stack([one, total - one])
    sizes = jnp.asarray(profile(amount, total, most, lean), jnp.int32)
    couples = (amount - 1) // 2
    donor, receiver = sizes[1:1 + 2 * couples:2], sizes[2:2 + 2 * couples:2]
    margin = jnp.minimum(donor - 1, most - receiver)
    moved = jax.random.randint(jax.random.fold_in(rng, 1), (couples,), 0, 1 << 20) % (margin + 1)
    sizes = sizes.at[1:1 + 2 * couples:2].set(donor - moved).at[2:2 + 2 * couples:2].set(receiver + moved)
    return sizes[jax.random.permutation(jax.random.fold_in(rng, 2), amount)]


def routed_block(own_key, own, number, rows, count, top, most, slope):
    ranking = jax.random.permutation(own_key, count)
    heavy_load, ordinary = load_shares(count, rows * top, most, slope, True), load_shares(count, rows * top, most, slope, False)
    places = jnp.arange(count)

    def named(lengths, rotation):
        used = int((lengths > 0).sum())
        fixed = max(1, used // 4)
        moved = fixed + (places - fixed + rotation * (used - fixed)) % max(1, count - fixed)
        return jnp.zeros((count,), jnp.int32).at[ranking[jnp.where(places < fixed, places, moved)]].set(jnp.asarray(lengths, jnp.int32))

    lengths = jnp.where(number % 4 == 0, named(heavy_load, number // 4), named(ordinary, number - number // 4 - 1))
    mixed = jax.random.permutation(jax.random.fold_in(own, 3), count)
    source_of, receiver = mixed[0:count // 2 * 2:2], mixed[1:count // 2 * 2:2]
    room = jnp.minimum(lengths[source_of] - 1, most - lengths[receiver]) // 2
    room = jnp.where((source_of == ranking[0]) | (receiver == ranking[0]) | (lengths[receiver] == 0), 0, jnp.maximum(room, 0))
    moved = jax.random.randint(jax.random.fold_in(own, 4), (count // 2,), 0, 1 << 20) % (room + 1)
    lengths = lengths.at[source_of].add(-moved).at[receiver].add(moved)
    members = jnp.searchsorted(jnp.cumsum(lengths), jnp.arange(rows * top), side="right").astype(jnp.int32)
    table = members.reshape(top, rows).T
    table = table[jax.random.permutation(jax.random.fold_in(own, 1), rows)]
    rotation = jax.random.randint(jax.random.fold_in(own, 2), (rows, 1), 0, top)
    return jnp.take_along_axis(table, (jnp.arange(top)[None, :] + rotation) % top, axis=1)


def load_shares(amount, total, most, lean, full):
    loads = [(1 << 20) // math.isqrt(standing ** lean) + 1 for standing in range(1, amount + 1)]
    largest = most if full else min(most, max(-(-total // amount), total * loads[0] // sum(loads)))
    least = 1 if total - largest >= amount - 1 else 0
    counts, spare = [largest] + [least] * (amount - 1), total - largest - least * (amount - 1)
    while spare > 0:
        candidates = [i for i in range(1, amount) if counts[i] < largest] or [i for i in range(1, amount) if counts[i] < most]
        mass, remaining = sum([loads[i] for i in candidates]), spare
        for i in candidates:
            more = min(most - counts[i], max(1, remaining * loads[i] // mass), spare)
            counts[i] = counts[i] + more
            spare = spare - more
    return np.array(counts)


def scatter_about(stream_key, shape, width, most, split=(), held_as=jnp.bfloat16):
    entries = jax.random.normal(stream_key, shape, jnp.float32) * width
    if len(split) > 0:
        entries = level_of(stream_key, shape, split, -0.22, 0.18) * entries
    return jnp.clip(entries, min=-most, max=most).astype(held_as)


def setup_inputs(seed: int = 0) -> dict:
    arg_keys = jax.random.split(jax.random.key(seed), 20)
    tokens = scatter_about(arg_keys[0], (TOKENS, D), 1.0, 6.0, ((0, 32),))
    cotangent = scatter_about(arg_keys[1], (TOKENS, D), 1.0, 6.0, ((0, 32),))
    routes_keys = jax.random.split(jax.random.fold_in(arg_keys[2], 1), TOKENS // TOK_DEV)
    routes_turns = jax.random.permutation(jax.random.fold_in(arg_keys[2], 3), TOKENS // TOK_DEV)
    routes = jax.vmap(lambda own, number: routed_block(jax.random.fold_in(arg_keys[2], 2), own, number, TOK_DEV, EXPERTS, TOPK, CAP, 1))(routes_keys, routes_turns).reshape((TOKENS, TOPK))
    doc_ids = jax.vmap(lambda own: jnp.searchsorted(jnp.cumsum(ragged(own, DOCS, TOK_DEV, TOK_DEV // 2, 2)), jnp.arange(TOK_DEV), side="right"))(jax.random.split(arg_keys[3], SEQS)).reshape((SEQS, TOK_DEV)).astype(jnp.int32)
    attn_weight = scatter_about(arg_keys[4], (4, D, D), D ** -0.5, 0.15625, ((1, 32),), jnp.float32)
    attn_momentum = scatter_about(arg_keys[5], (4, D, D), (TOKENS ** 0.5), 384.0, ((1, 32),), jnp.float32)
    attn_average = scatter_about(arg_keys[6], (4, D, D), D ** -0.5, 0.15625, ((1, 32),), jnp.float32)
    shared_weight = scatter_about(arg_keys[7], (3, D, FF), D ** -0.5, 0.15625, ((1, 32),), jnp.float32)
    shared_momentum = scatter_about(arg_keys[8], (3, D, FF), (TOKENS ** 0.5 / 2), 192.0, ((1, 32),), jnp.float32)
    shared_average = scatter_about(arg_keys[9], (3, D, FF), D ** -0.5, 0.15625, ((1, 32),), jnp.float32)
    router_weight = scatter_about(arg_keys[10], (D, EXPERTS), (4 * D) ** -0.5, 0.078125, ((0, 32),), jnp.float32)
    router_momentum = scatter_about(arg_keys[11], (D, EXPERTS), (3 * (TOKENS * TOPK // EXPERTS) ** 0.5), 512.0, ((0, 32),), jnp.float32)
    router_average = scatter_about(arg_keys[12], (D, EXPERTS), (4 * D) ** -0.5, 0.078125, ((0, 32),), jnp.float32)
    gain_weight = jnp.clip(1.0 + 0.1 * jax.random.normal(arg_keys[13], (2, D), jnp.float32), 0.5, 1.5)
    gain_momentum = scatter_about(arg_keys[14], (2, D), (TOKENS ** 0.5), 384.0, ((1, 32),), jnp.float32)
    gain_average = jnp.clip(1.0 + 0.18 * jax.random.normal(arg_keys[15], (2, D), jnp.float32), 0.1, 1.9)
    expert_weight = scatter_about(arg_keys[16], (EXPERTS, 3, D, FF), D ** -0.5, 0.15625, ((0, 8), (2, 4)), jnp.float32)
    expert_momentum = scatter_about(arg_keys[17], (EXPERTS, 3, D, FF), (EXPERT_ROWS ** 0.5 / 10), 16.0, ((0, 8), (2, 4)), jnp.float32)
    expert_average = scatter_about(arg_keys[18], (EXPERTS, 3, D, FF), D ** -0.5, 0.15625, ((0, 8), (2, 4)), jnp.float32)
    return {"tokens": tokens, "cotangent": cotangent, "routes": routes, "doc_ids": doc_ids, "attn_weight": attn_weight, "attn_momentum": attn_momentum, "attn_average": attn_average, "shared_weight": shared_weight, "shared_momentum": shared_momentum, "shared_average": shared_average, "router_weight": router_weight, "router_momentum": router_momentum, "router_average": router_average, "gain_weight": gain_weight, "gain_momentum": gain_momentum, "gain_average": gain_average, "expert_weight": expert_weight, "expert_momentum": expert_momentum, "expert_average": expert_average}


epsilon = 1e-06
momentum_decay = 0.9
masked_score = -1e+30
highest = lax.Precision.HIGHEST
rate_attn = 5e-05
rate_output = 0.0002
rate_shared = 0.0001
rate_router = 3e-05
rate_gain = 0.002
rate_expert = 0.0015

@jax.custom_vjp
def low(v):
    return lax.optimization_barrier(v.astype(jnp.bfloat16)).astype(jnp.float32)

@jax.custom_vjp
def low_back(v):
    return v

def low_keep(v):
    return (low(v), None)

def low_pass(kept, grad):
    return (grad,)

def back_keep(v):
    return (v, None)

def back_low(kept, grad):
    return (low(grad),)
low.defvjp(low_keep, low_pass)
low_back.defvjp(back_keep, back_low)

def swish(value_in):
    return value_in * jax.nn.sigmoid(value_in)

def rope_tables(length, size):
    half = size // 2
    freq = jnp.exp(jnp.arange(half, dtype=jnp.float32) * (-2.0 * math.log(10000.0) / size))
    angle = jnp.arange(length, dtype=jnp.float32)[:, None] * freq[None, :]
    cosine = jnp.concatenate([jnp.cos(angle), jnp.cos(angle)], -1)
    sine = jnp.concatenate([jnp.sin(angle), jnp.sin(angle)], -1)
    return (cosine, sine)

def rotate(heads_in, cosine, sine):
    half = heads_in.shape[-1] // 2
    turned = jnp.concatenate([-heads_in[..., half:], heads_in[..., :half]], -1)
    return heads_in * cosine[:, None, :] + turned * sine[:, None, :]

def destinations(routes_in, capacity, experts):
    flat = routes_in.reshape(-1)
    onehot = (flat[:, None] == jnp.arange(experts, dtype=jnp.int32)[None, :]).astype(jnp.int32)
    before = jnp.cumsum(onehot, 0) - onehot
    slot = lax.optimization_barrier(jnp.sum(before * onehot, 1)).astype(jnp.int32)
    return (flat * capacity + slot).astype(jnp.int32)

def rms_norm(value_in, gain):
    return value_in * lax.rsqrt(lax.optimization_barrier(jnp.mean(value_in * value_in, -1, keepdims=True)) + epsilon) * gain

def sequence(seq_in, documents, seq_routes, attn_w, shared_w, router_w, gain_w, expert_w):
    length = seq_in.shape[0]
    cosine, sine = rope_tables(length, HD)
    normed = low(rms_norm(seq_in, gain_w[0]))
    projected = jnp.einsum('ld,mde->mle', normed, attn_w[:3], precision=highest)
    query = low(rotate(low_back(projected[0]).reshape(length, HEADS, HD), cosine, sine))
    key_rot = low(rotate(low_back(projected[1]).reshape(length, HEADS, HD), cosine, sine))
    values = low(low_back(projected[2])).reshape(length, HEADS, HD)
    scores = jnp.einsum('ihd,jhd->hij', query, key_rot, precision=highest) * HD ** (-0.5)
    position = jnp.arange(length)
    allowed = (position[None, :] <= position[:, None]) & (documents[None, :] == documents[:, None])
    scores = low_back(jnp.where(allowed[None], scores, masked_score))
    attn_probs = jax.nn.softmax(scores, axis=-1)
    heads_out = jnp.einsum('hij,jhd->ihd', low(attn_probs), values, precision=highest).reshape(length, D)
    heads_out = low(low_back(heads_out))
    attn_out = low_back(jnp.dot(heads_out, attn_w[3], precision=highest))
    middle = seq_in + attn_out
    inner = low(rms_norm(middle, gain_w[1]))
    logits = jnp.dot(inner, router_w, precision=highest)
    chosen = jnp.take_along_axis(logits, seq_routes, 1)
    gate_probs = jax.nn.softmax(chosen, axis=-1)
    shared_gu = low_back(jnp.einsum('ld,mdf->mlf', inner, shared_w[:2], precision=highest))
    shared_hidden = low(swish(shared_gu[0]) * shared_gu[1])
    shared_out = low_back(jnp.einsum('lf,df->ld', shared_hidden, shared_w[2], precision=highest))
    target = destinations(seq_routes, CAP, EXPERTS)
    source = (jnp.arange(length * TOPK) // TOPK).astype(jnp.int32)
    outbound = jnp.zeros((EXPERTS * CAP, D), jnp.float32).at[target].set(inner[source])
    outbound = low_back(outbound).reshape(EXPERTS, CAP, D)
    expert_gu = low_back(jnp.einsum('ecd,emdf->mecf', outbound, expert_w[:, :2], precision=highest))
    expert_hidden = low(swish(expert_gu[0]) * expert_gu[1])
    expert_out = jnp.einsum('ecf,edf->ecd', expert_hidden, expert_w[:, 2], precision=highest)
    expert_out = low(low_back(expert_out)).reshape(EXPERTS * CAP, D)
    picked = expert_out[target].reshape(length, TOPK, D)
    routed = lax.optimization_barrier(jnp.sum(gate_probs[:, :, None] * picked, 1))
    branch = shared_out + routed
    first_mask = jnp.concatenate([jnp.ones((1,), bool), documents[1:] != documents[:-1]])
    kept_mask = 1.0 - first_mask.astype(jnp.float32)
    kept_count = jnp.sum(kept_mask)
    attn_rms = jnp.sqrt(jnp.sum(kept_mask[:, None] * attn_out * attn_out) / (kept_count * D))
    branch_rms = jnp.sqrt(jnp.sum(kept_mask[:, None] * branch * branch) / (kept_count * D))
    return (middle + branch, jnp.stack([attn_rms, branch_rms]))

def update(weight, moment, average, grad, rate):
    moment_new = momentum_decay * moment + grad
    weight_new = weight - rate * (grad + momentum_decay * moment_new)
    average_new = average + (weight_new - average) / (STEP + 1.0)
    return (weight_new, moment_new, average_new)

def reference(tokens, cotangent, routes, doc_ids, attn_weight, attn_momentum, attn_average, shared_weight, shared_momentum, shared_average, router_weight, router_momentum, router_average, gain_weight, gain_momentum, gain_average, expert_weight, expert_momentum, expert_average):
    route_seq = routes.reshape(SEQS, TOK_DEV, TOPK)

    def forward(inputs, attn_w, shared_w, router_w, gain_w, expert_w):
        attn_r = low(attn_w)
        shared_r = low(shared_w)
        router_r = low(router_w)
        gain_r = low(gain_w)
        expert_r = low(expert_w)

        def one_sequence(seq_in, documents, seq_routes):
            return sequence(seq_in, documents, seq_routes, attn_r, shared_r, router_r, gain_r, expert_r)
        checked = jax.checkpoint(one_sequence)

        def step_fn(carry, item):
            out_seq, stats = checked(item[0], item[1], item[2])
            return (carry, (out_seq, stats))
        carry_init = jnp.zeros((), jnp.float32)
        unused, (outs, stats) = lax.scan(step_fn, carry_init, (inputs.reshape(SEQS, TOK_DEV, D), doc_ids, route_seq))
        return (outs.reshape(TOKENS, D), stats)
    layer_out, pull, stats = jax.vjp(forward, tokens.astype(jnp.float32), attn_weight, shared_weight, router_weight, gain_weight, expert_weight, has_aux=True)
    input_grad, attn_grad, shared_grad, router_grad, gain_grad, expert_grad = pull(cotangent.astype(jnp.float32))
    attn_rates = jnp.array([rate_attn, rate_attn, rate_attn, rate_output], jnp.float32).reshape(4, 1, 1)
    attn_new, attn_moment, attn_mean = update(attn_weight, attn_momentum, attn_average, attn_grad, attn_rates)
    shared_new, shared_moment, shared_mean = update(shared_weight, shared_momentum, shared_average, shared_grad, rate_shared)
    router_new, router_moment, router_mean = update(router_weight, router_momentum, router_average, router_grad, rate_router)
    gain_new, gain_moment, gain_mean = update(gain_weight, gain_momentum, gain_average, gain_grad, rate_gain)
    expert_new, expert_moment, expert_mean = update(expert_weight, expert_momentum, expert_average, expert_grad, rate_expert)
    return (layer_out.astype(jnp.bfloat16), input_grad, attn_new, attn_moment, attn_mean, shared_new, shared_moment, shared_mean, router_new, router_moment, router_mean, gain_new, gain_moment, gain_mean, expert_new, expert_moment, expert_mean, stats)
```

```python
import math

import jax
import jax.numpy as jnp
from jax import lax
from jax.sharding import PartitionSpec as P

HEADS = 10
HD = 128
TOPK = 7
STEP = 3
BF = jnp.bfloat16
F32 = jnp.float32

epsilon = 1e-06
momentum_decay = 0.9
masked_score = -1e30
rate_attn = 5e-05
rate_output = 0.0002
rate_shared = 0.0001
rate_router = 3e-05
rate_gain = 0.002
rate_expert = 0.0015
ALL = ("dp", "expert")


def rope_tables(length, size):
    half = size // 2
    freq = jnp.exp(jnp.arange(half, dtype=F32) * (-2.0 * math.log(10000.0) / size))
    angle = jnp.arange(length, dtype=F32)[:, None] * freq[None, :]
    cosine = jnp.concatenate([jnp.cos(angle), jnp.cos(angle)], -1)
    sine = jnp.concatenate([jnp.sin(angle), jnp.sin(angle)], -1)
    return (cosine, sine)


def rotate(heads_in, cosine, sine):
    half = heads_in.shape[-1] // 2
    turned = jnp.concatenate([-heads_in[..., half:], heads_in[..., :half]], -1)
    return heads_in * cosine[:, None, :] + turned * sine[:, None, :]


def rotate_back(grads_in, cosine, sine):
    half = grads_in.shape[-1] // 2
    scaled = grads_in * sine[:, None, :]
    turned = jnp.concatenate([scaled[..., half:], -scaled[..., :half]], -1)
    return grads_in * cosine[:, None, :] + turned


def update(weight, moment, average, grad, rate):
    moment_new = momentum_decay * moment + grad
    weight_new = weight - rate * (grad + momentum_decay * moment_new)
    average_new = average + (weight_new - average) / (STEP + 1.0)
    return (weight_new, moment_new, average_new)


def mm(a, b):
    return jnp.dot(a, b, preferred_element_type=F32)


def mm_nt(a, b):
    return lax.dot_general(a, b, (((1,), (1,)), ((), ())), preferred_element_type=F32)


def mm_tn(a, b):
    return lax.dot_general(a, b, (((0,), (0,)), ((), ())), preferred_element_type=F32)


def body(
    tokens,
    cotangent,
    routes,
    doc_ids,
    attn_weight,
    attn_momentum,
    attn_average,
    shared_weight,
    shared_momentum,
    shared_average,
    router_weight,
    router_momentum,
    router_average,
    gain_weight,
    gain_momentum,
    gain_average,
    expert_weight,
    expert_momentum,
    expert_average,
):
    Z = lax.axis_size("dp")
    E = lax.axis_size("expert")
    L, D = tokens.shape
    rows_own = attn_weight.shape[1]
    local, _, deep, FF = expert_weight.shape
    experts = router_weight.shape[1]
    parts = Z // local
    FP = FF // parts
    FS = shared_weight.shape[2] // Z
    cap = min(L, (L * TOPK * 3 // (2 * experts) + 7) // 8 * 8)
    zi = lax.axis_index("dp")

    def swap_z(pieces):
        out = [pieces[0]]
        for k in range(1, Z):
            out.append(lax.ppermute(pieces[k], "dp", [(i, i ^ k) for i in range(Z)]))
        return out

    def gather_z(x):
        return swap_z([x] * Z)

    attn_rows = jnp.swapaxes(attn_weight, 0, 1).reshape(rows_own, 4 * D).astype(BF)
    extra = jnp.concatenate([router_weight, gain_weight.T], 1).astype(BF)
    extra = jnp.pad(extra, ((0, 0), (0, 128 - extra.shape[1])))
    packed = lax.all_gather(jnp.concatenate([attn_rows, extra], 1), ALL, axis=0, tiled=True)
    w_qkv = packed[:, : 3 * D]
    w_o = packed[:, 3 * D : 4 * D]
    router_w = packed[:, 4 * D : 4 * D + experts]
    gain_vals = packed[:, 4 * D + experts : 4 * D + experts + 2].astype(F32).T

    grad_in = jnp.stack(gather_z(cotangent))
    routes_z = jnp.stack(gather_z(routes))

    ew = expert_weight.astype(BF)
    expert_full = []
    for m in (0, 1, 2):
        w = ew[:, m].reshape(local, deep, parts, FP).transpose(0, 2, 1, 3).reshape(Z, deep, FP)
        expert_full.append(
            lax.all_to_all(w, "dp", split_axis=0, concat_axis=0, tiled=True).reshape(Z * deep, FP)
        )
    wg, wu, wd = expert_full

    sw = shared_weight.astype(BF).reshape(3, rows_own, Z, FS).transpose(2, 0, 1, 3)
    sw = lax.all_to_all(sw, "dp", split_axis=0, concat_axis=0, tiled=True)
    sw = lax.all_gather(sw, "expert", axis=0, tiled=False)
    shared_w = sw.transpose(2, 1, 0, 3, 4).reshape(3, D, FS)

    inputs = tokens.astype(F32)
    cosine, sine = rope_tables(L, HD)
    score_scale = HD ** (-0.5)
    documents = doc_ids[0]
    position = jnp.arange(L)
    allowed = (
        (position[None, :] <= position[:, None]) & (documents[None, :] == documents[:, None])
    )[None]
    inv_first = lax.rsqrt(jnp.mean(inputs * inputs, -1, keepdims=True) + epsilon)
    unit_first = inputs * inv_first
    normed = (unit_first * gain_vals[0]).astype(BF)
    projected = mm(normed, w_qkv)
    query = rotate(projected[:, :D].reshape(L, HEADS, HD), cosine, sine).astype(BF)
    key_rot = rotate(projected[:, D : 2 * D].reshape(L, HEADS, HD), cosine, sine).astype(BF)
    values = projected[:, 2 * D :].astype(BF).reshape(L, HEADS, HD)
    raw = jnp.einsum("ihd,jhd->hij", query, key_rot, preferred_element_type=F32) * score_scale
    scores = jnp.where(allowed, raw, masked_score)
    row_max = jnp.max(scores, -1, keepdims=True)
    exponent = jnp.exp(scores - row_max)
    attn_probs = exponent / jnp.sum(exponent, -1, keepdims=True)
    probs_low = attn_probs.astype(BF)
    heads_out = jnp.einsum("hij,jhd->ihd", probs_low, values, preferred_element_type=F32)
    heads_out = heads_out.reshape(L, D).astype(BF)
    attn_out = mm(heads_out, w_o)
    middle = inputs + attn_out
    inv_second = lax.rsqrt(jnp.mean(middle * middle, -1, keepdims=True) + epsilon)
    unit_second = middle * inv_second
    inner = (unit_second * gain_vals[1]).astype(BF)

    inner_z = jnp.stack(gather_z(inner))
    hot = jnp.sum(
        (routes_z[:, :, :, None] == jnp.arange(experts, dtype=jnp.int32)).astype(F32), 2
    )
    before = (position[None, :] < position[:, None]).astype(BF)
    rank = jnp.einsum("tu,sux->stx", before, hot.astype(BF), preferred_element_type=F32)
    first = zi // parts
    mine = jnp.arange(E) * local + first
    pick = (jnp.arange(experts)[:, None] == mine[None, :]).astype(F32)
    hot_mine = jnp.einsum("stx,xe->est", hot, pick)
    rank_mine = jnp.einsum("stx,xe->est", rank, pick, precision=lax.Precision.HIGHEST)
    place = (
        (rank_mine[:, :, None, :] == jnp.arange(cap, dtype=F32)[None, None, :, None])
        & (hot_mine[:, :, None, :] > 0.5)
    ).astype(BF)

    logits = jnp.einsum("std,dx->stx", inner_z, router_w, preferred_element_type=F32)
    chosen = jnp.where(hot > 0.5, logits, masked_score)
    chosen_max = jnp.max(chosen, -1, keepdims=True)
    chosen_exp = jnp.where(hot > 0.5, jnp.exp(chosen - chosen_max), 0.0)
    gates = chosen_exp / jnp.sum(chosen_exp, -1, keepdims=True)
    gates_mine = jnp.einsum("stx,xe->est", gates, pick, precision=lax.Precision.HIGHEST)
    gate_rows = jnp.sum(place.astype(F32) * gates_mine[:, :, None, :], -1)

    def dispatch(x):
        rows = jnp.einsum("esct,std->escd", place, x, preferred_element_type=F32).astype(BF)
        return lax.all_to_all(rows, "expert", split_axis=0, concat_axis=0, tiled=True).reshape(
            E * Z * cap, D
        )

    def collect(rows, add):
        back = lax.all_to_all(
            rows.reshape(E, Z, cap, D), "expert", split_axis=0, concat_axis=0, tiled=True
        )
        total = jnp.einsum("esct,escd->std", place, back, preferred_element_type=F32) + add
        total = total.astype(BF)
        got = swap_z([total[k] for k in range(Z)])
        return sum(g.astype(F32) for g in got)

    grad_rows = dispatch(grad_in)
    rows = dispatch(inner_z)
    gate_col = lax.all_to_all(gate_rows, "expert", split_axis=0, concat_axis=0, tiled=True)
    gate_col = gate_col.reshape(E * Z * cap, 1)

    eg = mm(rows, wg)
    eu = mm(rows, wu)
    sig = jax.nn.sigmoid(eg)
    silu = eg * sig
    hidden = silu * eu
    gated = (gate_col * hidden).astype(BF)
    plain_grad = mm(grad_rows, wd)
    gate_grad = jnp.sum(hidden * plain_grad, -1)
    hidden_grad = gate_col * plain_grad
    eg_grad = (hidden_grad * eu * sig * (1.0 + eg * (1.0 - sig))).astype(BF)
    eu_grad = (hidden_grad * silu).astype(BF)
    rows_grad = (mm_nt(eg_grad, wg) + mm_nt(eu_grad, wu)).astype(BF)
    routed_rows = mm_nt(gated, wd).astype(BF)

    flat_inner = inner_z.reshape(Z * L, D)
    flat_grad = grad_in.reshape(Z * L, D)
    sg = mm(flat_inner, shared_w[0])
    su = mm(flat_inner, shared_w[1])
    ssig = jax.nn.sigmoid(sg)
    ssilu = sg * ssig
    shared_hidden = (ssilu * su).astype(BF)
    shared_out = mm_nt(shared_hidden, shared_w[2])
    shared_hidden_grad = mm(flat_grad, shared_w[2])
    sg_grad = (shared_hidden_grad * su * ssig * (1.0 + sg * (1.0 - ssig))).astype(BF)
    su_grad = (shared_hidden_grad * ssilu).astype(BF)
    shared_back = mm_nt(sg_grad, shared_w[0]) + mm_nt(su_grad, shared_w[1])
    shared_grads = jnp.stack(
        [mm_tn(flat_inner, sg_grad), mm_tn(flat_inner, su_grad), mm_tn(flat_grad, shared_hidden)]
    ).astype(BF)

    inner_grad = collect(rows_grad, shared_back.reshape(Z, L, D))
    branch = collect(routed_rows, shared_out.reshape(Z, L, D))

    gate_grad_back = lax.all_to_all(
        gate_grad.reshape(E, Z, cap), "expert", split_axis=0, concat_axis=0, tiled=True
    )
    gate_grad_mine = jnp.sum(place.astype(F32) * gate_grad_back[:, :, :, None], 2)
    gate_grad_z = jnp.einsum(
        "est,xe->stx", gate_grad_mine, pick, precision=lax.Precision.HIGHEST
    )
    got = swap_z([gate_grad_z[k] for k in range(Z)])
    gate_grad_own = sum(got)
    gates_own = gates[0]
    logit_grad = gates_own * (
        gate_grad_own - jnp.sum(gates_own * gate_grad_own, -1, keepdims=True)
    )
    router_grad = mm_tn(inner.astype(F32), logit_grad)
    router_back = mm_nt(logit_grad, router_w.astype(F32))
    inner_grad = inner_grad + router_back

    layer_out = (middle + branch).astype(BF)
    first_mask = jnp.concatenate([jnp.ones((1,), bool), documents[1:] != documents[:-1]])
    kept_mask = 1.0 - first_mask.astype(F32)
    kept_total = jnp.sum(kept_mask) * D
    attn_rms = jnp.sqrt(jnp.sum(kept_mask[:, None] * attn_out * attn_out) / kept_total)
    branch_rms = jnp.sqrt(jnp.sum(kept_mask[:, None] * branch * branch) / kept_total)
    sublayer_rms = jnp.stack([attn_rms, branch_rms])[None, :]

    upstream = cotangent.astype(F32)
    scaled_second = inner_grad * gain_vals[1]
    second_gain_grad = jnp.sum(inner_grad * unit_second, 0)
    middle_grad = upstream + inv_second * (
        scaled_second - unit_second * jnp.mean(scaled_second * unit_second, -1, keepdims=True)
    )
    attn_grad = middle_grad.astype(BF)
    output_grad = mm_tn(heads_out, attn_grad)
    heads_grad = mm_nt(attn_grad, w_o).astype(BF).reshape(L, HEADS, HD)
    value_grad = jnp.einsum(
        "hij,ihd->jhd", probs_low, heads_grad, preferred_element_type=F32
    ).astype(BF)
    prob_grad = jnp.einsum("ihd,jhd->hij", heads_grad, values, preferred_element_type=F32)
    score_grad = (
        attn_probs * (prob_grad - jnp.sum(attn_probs * prob_grad, -1, keepdims=True))
    ).astype(BF)
    query_grad = (
        jnp.einsum("hij,jhd->ihd", score_grad, key_rot, preferred_element_type=F32) * score_scale
    )
    query_grad = rotate_back(query_grad, cosine, sine).astype(BF)
    key_grad = (
        jnp.einsum("hij,ihd->jhd", score_grad, query, preferred_element_type=F32) * score_scale
    )
    key_grad = rotate_back(key_grad, cosine, sine).astype(BF)
    proj_grad = jnp.concatenate(
        [query_grad.reshape(L, D), key_grad.reshape(L, D), value_grad.reshape(L, D)], 1
    )
    qkv_grad = mm_tn(normed, proj_grad)
    normed_grad = mm_nt(proj_grad, w_qkv)
    scaled_first = normed_grad * gain_vals[0]
    first_gain_grad = jnp.sum(normed_grad * unit_first, 0)
    input_grad = middle_grad + inv_first * (
        scaled_first - unit_first * jnp.mean(scaled_first * unit_first, -1, keepdims=True)
    )

    down_grad = mm_tn(grad_rows, gated).astype(BF)
    gate_w_grad = mm_tn(rows, eg_grad).astype(BF)
    up_w_grad = mm_tn(rows, eu_grad).astype(BF)
    sums = []
    for g in (gate_w_grad, up_w_grad, down_grad):
        g = lax.all_to_all(g.reshape(Z, deep, FP), "dp", split_axis=0, concat_axis=0, tiled=True)
        g = g.reshape(local, parts, deep, FP).transpose(0, 2, 1, 3).reshape(local, deep, FF)
        sums.append(g.astype(F32))
    expert_sum = jnp.stack(sums, 1)

    gain_all = jnp.stack([first_gain_grad, second_gain_grad], 1)
    pad = jnp.zeros((D, 128 - experts - 2), F32)
    attn_all = jnp.concatenate([qkv_grad, output_grad, router_grad, gain_all, pad], 1).astype(BF)
    attn_own = lax.psum_scatter(attn_all, ALL, scatter_dimension=0, tiled=True).astype(F32)
    attn_sum = jnp.swapaxes(attn_own[:, : 4 * D].reshape(rows_own, 4, D), 0, 1)
    router_sum = attn_own[:, 4 * D : 4 * D + experts]
    gain_sum = attn_own[:, 4 * D + experts : 4 * D + experts + 2].T

    sgr = shared_grads.reshape(3, Z, E, rows_own, FS).transpose(2, 1, 0, 3, 4)
    sgr = lax.psum_scatter(sgr, "expert", scatter_dimension=0, tiled=False)
    sgr = lax.all_to_all(sgr, "dp", split_axis=0, concat_axis=0, tiled=True)
    shared_sum = sgr.transpose(1, 2, 0, 3).reshape(3, rows_own, Z * FS).astype(F32)

    attn_rates = jnp.array([rate_attn, rate_attn, rate_attn, rate_output], F32).reshape(4, 1, 1)
    return (
        layer_out,
        input_grad,
        *update(attn_weight, attn_momentum, attn_average, attn_sum, attn_rates),
        *update(shared_weight, shared_momentum, shared_average, shared_sum, rate_shared),
        *update(router_weight, router_momentum, router_average, router_sum, rate_router),
        *update(gain_weight, gain_momentum, gain_average, gain_sum, rate_gain),
        *update(expert_weight, expert_momentum, expert_average, expert_sum, rate_expert),
        sublayer_rms,
    )


def solution(mesh):
    rows = P(ALL, None)
    middle = P(None, ALL, None)
    gains = P(None, ALL)
    routed = P("expert", None, "dp", None)
    weights = (middle,) * 6 + (rows,) * 3 + (gains,) * 3 + (routed,) * 3
    return jax.shard_map(
        body,
        mesh=mesh,
        in_specs=(rows,) * 4 + weights,
        out_specs=(rows,) * 2 + weights + (rows,),
        check_vma=False,
    )
```

```python
import functools
import math

import jax
import jax.numpy as jnp
from jax import lax
from jax.experimental import pallas as pl
from jax.experimental.pallas import tpu as pltpu
from jax.sharding import PartitionSpec as P

HEADS = 10
HD = 128
TOPK = 7
STEP = 3
BF = jnp.bfloat16
F32 = jnp.float32

epsilon = 1e-06
momentum_decay = 0.9
masked_score = -1e30
rate_attn = 5e-05
rate_output = 0.0002
rate_shared = 0.0001
rate_router = 3e-05
rate_gain = 0.002
rate_expert = 0.0015
ALL = ("dp", "expert")


def rope_tables(length, size):
    half = size // 2
    freq = jnp.exp(jnp.arange(half, dtype=F32) * (-2.0 * math.log(10000.0) / size))
    angle = jnp.arange(length, dtype=F32)[:, None] * freq[None, :]
    cosine = jnp.concatenate([jnp.cos(angle), jnp.cos(angle)], -1)
    sine = jnp.concatenate([jnp.sin(angle), jnp.sin(angle)], -1)
    return (cosine, sine)


def update(weight, moment, average, grad, rate):
    moment_new = momentum_decay * moment + grad
    weight_new = weight - rate * (grad + momentum_decay * moment_new)
    average_new = average + (weight_new - average) / (STEP + 1.0)
    return (weight_new, moment_new, average_new)


def mm(a, b):
    return jnp.dot(a, b, preferred_element_type=F32)


def mm_nt(a, b):
    return lax.dot_general(a, b, (((1,), (1,)), ((), ())), preferred_element_type=F32)


def mm_tn(a, b):
    return lax.dot_general(a, b, (((0,), (0,)), ((), ())), preferred_element_type=F32)


def attend_probs(heads_ref, doc_row_ref, doc_col_ref, block):
    share = heads_ref.shape[2] // HD

    def head(b):
        return heads_ref[b // share, :, (b % share) * HD : (b % share + 1) * HD]

    length = heads_ref.shape[1]
    row = lax.broadcasted_iota(jnp.int32, (length, length), 0)
    col = lax.broadcasted_iota(jnp.int32, (length, length), 1)
    allowed = (col <= row) & (doc_row_ref[...] == doc_col_ref[...])
    query, key = head(block), head(HEADS + block)
    scores = jnp.where(allowed, mm_nt(query, key) * HD ** (-0.5), masked_score)
    exponent = jnp.exp(scores - jnp.max(scores, -1, keepdims=True))
    probs = exponent / jnp.sum(exponent, -1, keepdims=True)
    return query, key, head(2 * HEADS + block), probs


def attend_kernel(heads_ref, doc_row_ref, doc_col_ref, out_ref):
    for h in range(HEADS):
        _, _, value, probs = attend_probs(heads_ref, doc_row_ref, doc_col_ref, h)
        out_ref[:, h * HD : (h + 1) * HD] = mm(probs.astype(BF), value).astype(BF)


def attend(heads, doc_row, doc_col):
    return pl.pallas_call(
        attend_kernel,
        out_shape=jax.ShapeDtypeStruct((heads.shape[1], HEADS * HD), BF),
        compiler_params=pltpu.CompilerParams(vmem_limit_bytes=24 << 20),
        name="attend",
    )(heads, doc_row, doc_col)


def out_kernel(heads_ref, tokens_ref, w_ref, gain_ref, middle_ref, inner_ref, square_ref):
    attn_out = mm(heads_ref[...], w_ref[...])
    middle = tokens_ref[...].astype(F32) + attn_out
    scale = lax.rsqrt(jnp.mean(middle * middle, -1, keepdims=True) + epsilon)
    middle_ref[...] = middle
    inner_ref[...] = (middle * scale * gain_ref[...]).astype(BF)
    square = jnp.sum(attn_out * attn_out, -1, keepdims=True)
    square_ref[...] = jnp.broadcast_to(square, square_ref.shape)


def project_out(heads_out, tokens, packed, gain):
    length, width = tokens.shape
    return pl.pallas_call(
        out_kernel,
        grid=(1,),
        in_specs=[
            pl.BlockSpec((length, width), lambda i: (0, 0)),
            pl.BlockSpec((length, width), lambda i: (0, 0)),
            pl.BlockSpec((width, width), lambda i: (0, 0)),
            pl.BlockSpec((1, width), lambda i: (0, 0)),
        ],
        out_specs=[
            pl.BlockSpec((length, width), lambda i: (0, 0)),
            pl.BlockSpec((length, width), lambda i: (0, 0)),
            pl.BlockSpec((length, 128), lambda i: (0, 0)),
        ],
        out_shape=[
            jax.ShapeDtypeStruct((length, width), F32),
            jax.ShapeDtypeStruct((length, width), BF),
            jax.ShapeDtypeStruct((length, 128), F32),
        ],
        compiler_params=pltpu.CompilerParams(vmem_limit_bytes=24 << 20),
        name="project_out",
    )(heads_out, tokens, packed, gain)


def attend_back_kernel(
    ig_ref, g_ref, middle_ref, w_ref, gain_ref, heads_ref, doc_row_ref, doc_col_ref,
    cos_ref, sin_ref, mg_ref, ag_ref, gain_out, out_ref, hg_ref
):
    grad = ig_ref[...]
    middle = middle_ref[...]
    scale = lax.rsqrt(jnp.mean(middle * middle, -1, keepdims=True) + epsilon)
    unit = middle * scale
    scaled = grad * gain_ref[...]
    gain_out[...] = jnp.sum(grad * unit, 0, keepdims=True)
    middle_grad = g_ref[...].astype(F32) + scale * (
        scaled - unit * jnp.mean(scaled * unit, -1, keepdims=True)
    )
    mg_ref[...] = middle_grad
    attn_grad = middle_grad.astype(BF)
    ag_ref[...] = attn_grad
    hg_ref[...] = mm_nt(attn_grad, w_ref[...]).astype(BF)
    share = heads_ref.shape[2] // HD

    def put(b, value):
        out_ref[b // share, :, (b % share) * HD : (b % share + 1) * HD] = value

    lane = lax.broadcasted_iota(jnp.int32, cos_ref.shape, 1)
    sign_sin = jnp.where(lane < HD // 2, -sin_ref[...], sin_ref[...])

    def rotate_back(z):
        return (z * cos_ref[...] + pltpu.roll(z * sign_sin, HD // 2, 1)).astype(BF)

    for h in range(HEADS):
        query, key, value, probs = attend_probs(heads_ref, doc_row_ref, doc_col_ref, h)
        out_grad = hg_ref[:, h * HD : (h + 1) * HD]
        prob_grad = mm_nt(out_grad, value)
        score_grad = (
            probs * (prob_grad - jnp.sum(probs * prob_grad, -1, keepdims=True))
        ).astype(BF)
        put(h, rotate_back(mm(score_grad, key) * HD ** (-0.5)))
        put(HEADS + h, rotate_back(mm_tn(score_grad, query) * HD ** (-0.5)))
        put(2 * HEADS + h, mm_tn(probs.astype(BF), out_grad).astype(BF))
    for b in range(3 * HEADS, heads_ref.shape[0] * share):
        put(b, jnp.zeros((heads_ref.shape[1], HD), BF))


def attend_back(grad, cotangent, middle, packed, gain, heads, doc_row, doc_col, cosine, sine):
    length, width = middle.shape
    whole = pl.BlockSpec((length, width), lambda i: (0, 0))
    table = pl.BlockSpec((length, HD), lambda i: (0, 0))
    row = pl.BlockSpec((1, width), lambda i: (0, 0))
    blocks = pl.BlockSpec(heads.shape, lambda i: (0, 0, 0))
    return pl.pallas_call(
        attend_back_kernel,
        grid=(1,),
        in_specs=[
            whole,
            whole,
            whole,
            pl.BlockSpec((width, width), lambda i: (0, 0)),
            row,
            blocks,
            pl.BlockSpec((1, length), lambda i: (0, 0)),
            pl.BlockSpec((length, 1), lambda i: (0, 0)),
            table,
            table,
        ],
        out_specs=[whole, whole, row, blocks],
        out_shape=[
            jax.ShapeDtypeStruct((length, width), F32),
            jax.ShapeDtypeStruct((length, width), BF),
            jax.ShapeDtypeStruct((1, width), F32),
            jax.ShapeDtypeStruct(heads.shape, BF),
        ],
        scratch_shapes=[pltpu.VMEM((length, width), BF)],
        compiler_params=pltpu.CompilerParams(vmem_limit_bytes=32 << 20),
        name="attend_back",
    )(grad, cotangent, middle, packed, gain, heads, doc_row, doc_col, cosine, sine)


def load_pieces(zi, pieces, dest, sem):
    depth = pieces[0].shape[1]
    copies = [
        pltpu.make_async_copy(
            piece,
            dest.at[:, pl.ds(pl.multiple_of((zi ^ k) * depth, 16), depth)],
            sem.at[k],
        )
        for k, piece in enumerate(pieces)
    ]
    for copy in copies:
        copy.start()
    for copy in copies:
        copy.wait()


def front_kernel(count, place_ref, x_ref, hot_ref, router_ref, *rest):
    pieces = rest[:count]
    eg_ref, eu_ref, gated_ref, gate_ref, w_ref, sem = rest[count:]

    @pl.when(pl.program_id(0) == 0)
    def _():
        half = count // 2
        load_pieces(place_ref[0], pieces[:half], w_ref.at[pl.ds(0, 1)], sem)
        load_pieces(place_ref[0], pieces[half:], w_ref.at[pl.ds(1, 1)], sem)

    x = x_ref[...]
    hot = hot_ref[...].astype(F32) > 0.5
    chosen = jnp.where(hot, mm(x, router_ref[...]), masked_score)
    top = jnp.max(chosen, -1, keepdims=True)
    exponent = jnp.where(hot, jnp.exp(chosen - top), 0.0)
    lane = lax.broadcasted_iota(jnp.int32, exponent.shape, 1)
    own = jnp.sum(jnp.where(lane == place_ref[1], exponent, 0.0), -1, keepdims=True)
    gate = own / jnp.maximum(jnp.sum(exponent, -1, keepdims=True), 0.5)
    eg = mm(x, w_ref[0])
    eu = mm(x, w_ref[1])
    eg_ref[...] = eg
    eu_ref[...] = eu
    gated_ref[...] = (gate * (eg * jax.nn.sigmoid(eg) * eu)).astype(BF)
    gate_ref[...] = jnp.broadcast_to(gate, gate_ref.shape)


def tile_of(count):
    return next(t for t in (256, 192, 128, 64, 48, 16, 8) if count % t == 0)


def expert_front(place, rows, grads_hot, router, pieces):
    count, width = rows.shape
    hidden = pieces[0].shape[2]
    tile = tile_of(count)
    extra = grads_hot.shape[1] - width
    flops = 4 * count * width * hidden
    return pl.pallas_call(
        functools.partial(front_kernel, len(pieces)),
        grid_spec=pltpu.PrefetchScalarGridSpec(
            num_scalar_prefetch=1,
            grid=(count // tile,),
            in_specs=[
                pl.BlockSpec((tile, width), lambda i, p: (i, 0)),
                pl.BlockSpec((tile, extra), lambda i, p: (i, width // extra)),
                pl.BlockSpec((width, extra), lambda i, p: (0, 0)),
            ]
            + [pl.BlockSpec(memory_space=pl.ANY)] * len(pieces),
            out_specs=[pl.BlockSpec((tile, hidden), lambda i, p: (i, 0))] * 3
            + [pl.BlockSpec((tile, 128), lambda i, p: (i, 0))],
            scratch_shapes=[
                pltpu.VMEM((2, width, hidden), BF),
                pltpu.SemaphoreType.DMA((len(pieces),)),
            ],
        ),
        out_shape=[
            jax.ShapeDtypeStruct((count, hidden), F32),
            jax.ShapeDtypeStruct((count, hidden), F32),
            jax.ShapeDtypeStruct((count, hidden), BF),
            jax.ShapeDtypeStruct((count, 128), F32),
        ],
        cost_estimate=pl.CostEstimate(
            flops=flops, bytes_accessed=12 * count * hidden, transcendentals=0
        ),
        compiler_params=pltpu.CompilerParams(vmem_limit_bytes=40 << 20),
        name="expert_front",
    )(place, rows, grads_hot, router, *pieces)


def back_kernel(count, place_ref, g_ref, eg_ref, eu_ref, gated_ref, gate_ref, *rest):
    gate_w, up_w, down = rest[:count], rest[count : 2 * count], rest[2 * count : 3 * count]
    rows_ref, routed_ref, egg_ref, eug_ref, gg_ref, w_ref, wd_ref, sem = rest[3 * count :]

    @pl.when(pl.program_id(0) == 0)
    def _():
        load_pieces(place_ref[0], down, wd_ref, sem)
        load_pieces(place_ref[0], gate_w, w_ref.at[pl.ds(0, 1)], sem)
        load_pieces(place_ref[0], up_w, w_ref.at[pl.ds(1, 1)], sem)

    eg = eg_ref[...]
    eu = eu_ref[...]
    sig = jax.nn.sigmoid(eg)
    silu = eg * sig
    plain = mm(g_ref[...], wd_ref[0])
    gate_grad = jnp.sum(silu * eu * plain, -1, keepdims=True)
    gg_ref[0] = jnp.broadcast_to(gate_grad, (gate_grad.shape[0], 128)).T[:8]
    grad = gate_ref[:, :1] * plain
    eg_grad = (grad * eu * sig * (1.0 + eg * (1.0 - sig))).astype(BF)
    eu_grad = (grad * silu).astype(BF)
    egg_ref[...] = eg_grad
    eug_ref[...] = eu_grad
    rows_ref[...] = (mm_nt(eg_grad, w_ref[0]) + mm_nt(eu_grad, w_ref[1])).astype(BF)
    routed_ref[...] = mm_nt(gated_ref[...], wd_ref[0]).astype(BF)


def expert_back(place, grads_hot, eg, eu, gated, gate, front, down, tile):
    count, hidden = eg.shape
    deep = front[0].shape[1]
    width = deep * len(down)
    wide = pl.BlockSpec((tile, width), lambda i, p: (i, 0))
    thin = pl.BlockSpec((tile, hidden), lambda i, p: (i, 0))
    lanes = pl.BlockSpec((tile, 128), lambda i, p: (i, 0))
    return pl.pallas_call(
        functools.partial(back_kernel, len(down)),
        grid_spec=pltpu.PrefetchScalarGridSpec(
            num_scalar_prefetch=1,
            grid=(count // tile,),
            in_specs=[wide, thin, thin, thin, lanes]
            + [pl.BlockSpec(memory_space=pl.ANY)] * (3 * len(down)),
            out_specs=[wide, wide, thin, thin, pl.BlockSpec((1, 8, tile), lambda i, p: (i, 0, 0))],
            scratch_shapes=[
                pltpu.VMEM((2, width, hidden), BF),
                pltpu.VMEM((1, width, hidden), BF),
                pltpu.SemaphoreType.DMA((len(down),)),
            ],
        ),
        out_shape=[
            jax.ShapeDtypeStruct((count, width), BF),
            jax.ShapeDtypeStruct((count, width), BF),
            jax.ShapeDtypeStruct((count, hidden), BF),
            jax.ShapeDtypeStruct((count, hidden), BF),
            jax.ShapeDtypeStruct((count // tile, 8, tile), F32),
        ],
        cost_estimate=pl.CostEstimate(
            flops=8 * count * width * hidden,
            bytes_accessed=16 * count * hidden,
            transcendentals=0,
        ),
        compiler_params=pltpu.CompilerParams(vmem_limit_bytes=48 << 20),
        name="expert_back",
    )(place, grads_hot, eg, eu, gated, gate, *front, *down)


def weight_grads(x, ys, width):
    count = x.shape[0]
    hidden = ys[0].shape[1]
    tile = 256
    return pl.pallas_call(
        grads_body(len(ys)),
        grid=(width // tile,),
        in_specs=[pl.BlockSpec((count, tile), lambda i: (0, i))]
        + [pl.BlockSpec((count, hidden), lambda i: (0, 0))] * len(ys),
        out_specs=pl.BlockSpec((len(ys), tile, hidden), lambda i: (0, i, 0)),
        out_shape=jax.ShapeDtypeStruct((len(ys), width, hidden), BF),
        cost_estimate=pl.CostEstimate(
            flops=2 * len(ys) * count * width * hidden,
            bytes_accessed=2 * count * (width + hidden),
            transcendentals=0,
        ),
        compiler_params=pltpu.CompilerParams(vmem_limit_bytes=40 << 20),
        name="weight_grads",
    )(x, *ys)


def grads_body(many):
    def kernel(x_ref, *rest):
        x = x_ref[...]
        for i in range(many):
            rest[many][i] = mm_tn(x, rest[i][...]).astype(BF)

    return kernel


def update_kernel(place_ref, w_ref, m_ref, a_ref, g_ref, *rest):
    w_out, m_out, a_out = rest[-3:]
    new = update(w_ref[0, 0], m_ref[0, 0], a_ref[0, 0], g_ref[0].astype(F32), rate_expert)
    w_out[0, 0], m_out[0, 0], a_out[0, 0] = new


def update_part(owned, so_far, grad, low, place):
    count, deep, width = grad.shape
    tile = deep // 2
    state = pl.BlockSpec((1, 1, tile, width), lambda m, t, p: (p[0], low + m, t, 0))
    moved = 6 * 4 * grad.size + 2 * grad.size
    return pl.pallas_call(
        update_kernel,
        grid_spec=pltpu.PrefetchScalarGridSpec(
            num_scalar_prefetch=1,
            grid=(count, deep // tile),
            in_specs=[state] * 3
            + [pl.BlockSpec((1, tile, width), lambda m, t, p: (m, t, 0))]
            + [pl.BlockSpec(memory_space=pl.ANY)] * len(so_far),
            out_specs=[state] * 3,
        ),
        out_shape=[jax.ShapeDtypeStruct(x.shape, x.dtype) for x in owned],
        input_output_aliases={5 + i: i for i in range(len(so_far))},
        cost_estimate=pl.CostEstimate(
            flops=8 * grad.size, bytes_accessed=moved, transcendentals=0
        ),
        compiler_params=pltpu.CompilerParams(vmem_limit_bytes=60 << 20),
        name="update_part",
    )(jnp.reshape(place, (1,)).astype(jnp.int32), *owned, grad, *so_far)


def body(
    tokens,
    cotangent,
    routes,
    doc_ids,
    attn_weight,
    attn_momentum,
    attn_average,
    shared_weight,
    shared_momentum,
    shared_average,
    router_weight,
    router_momentum,
    router_average,
    gain_weight,
    gain_momentum,
    gain_average,
    expert_weight,
    expert_momentum,
    expert_average,
):
    Z = lax.axis_size("dp")
    E = lax.axis_size("expert")
    L, D = tokens.shape
    rows_own = attn_weight.shape[1]
    local, _, deep, FF = expert_weight.shape
    experts = router_weight.shape[1]
    parts = Z // local
    FP = FF // parts
    FS = shared_weight.shape[2] // Z
    cap = min(L, (L * TOPK * 3 // (2 * experts) + 7) // 8 * 8)
    zi = lax.axis_index("dp")

    def swap_z(pieces):
        out = [pieces[0]]
        for k in range(1, Z):
            out.append(lax.ppermute(pieces[k], "dp", [(i, i ^ k) for i in range(Z)]))
        return out

    strides = [1 << b for b in range(Z.bit_length() - 1)][::-1]
    offs = [0]
    for stride in strides:
        offs = offs + [o ^ stride for o in offs]

    def gather_z(x, then=()):
        held = x[None]
        for step, stride in enumerate(strides):
            if step > 0 and then:
                held = after(held, *then)
            got = lax.ppermute(held, "dp", [(i, i ^ stride) for i in range(Z)])
            held = jnp.concatenate([held, got], 0)
        return held

    def reduce_z(x):
        for stride in strides[::-1]:
            keep, send = jnp.split(x, 2, 0)
            got = lax.ppermute(send, "dp", [(i, i ^ stride) for i in range(Z)])
            total = keep.astype(F32) + got.astype(F32)
            x = total.astype(BF)
        return total[0]

    R = rows_own
    ei = lax.axis_index("expert")

    def after(x, *needed):
        return lax.optimization_barrier((x,) + needed)[0]

    blocks = 3 * D // HD
    share = -(-blocks // E)
    wide = share * HD
    gain_low = gain_weight.astype(BF).astype(F32)
    folded = (attn_weight[:3].astype(BF).astype(F32) * gain_low[0][None, :, None]).astype(BF)
    folded = jnp.swapaxes(folded, 0, 1).reshape(R, 3 * D)
    folded = jnp.pad(folded, ((0, 0), (0, E * wide - 3 * D)))
    folded = jnp.swapaxes(folded.reshape(R, E, wide), 0, 1)
    folded = jnp.broadcast_to(folded[None], (Z, E, R, wide)).reshape(Z * E, R, wide)
    w_proj = lax.all_to_all(folded, ALL, split_axis=0, concat_axis=0, tiled=True)
    w_proj = w_proj.reshape(D, wide)

    inputs = tokens.astype(F32)
    inv_first = lax.rsqrt(jnp.mean(inputs * inputs, -1, keepdims=True) + epsilon)
    unit_first = inputs * inv_first
    unit_all = lax.all_gather(unit_first.astype(BF), "expert", axis=0, tiled=True)

    extra = jnp.concatenate([router_weight, gain_weight[1:].T], 1).astype(BF)
    extra = jnp.pad(extra, ((0, 0), (0, 128 - extra.shape[1])))
    packed = jnp.concatenate([attn_weight[3].astype(BF), extra], 1)
    packed = lax.all_gather(gather_z(packed), "expert", axis=0, tiled=False)
    full = jnp.zeros((Z, E, R, D + 128), BF)
    for k, o in enumerate(offs):
        full = lax.dynamic_update_slice(full, packed[:, k][None], (zi ^ o, 0, 0, 0))
    packed = full.reshape(D, D + 128)
    w_o = packed[:, :D]
    router_w = packed[:, D : D + experts]
    gain_second = packed[:, D + experts].astype(F32)

    def piece_of(k, low, high):
        there = zi ^ k
        w = lax.dynamic_slice(
            expert_weight,
            (there // parts, low, 0, (there % parts) * FP),
            (1, high - low, deep, FP),
        )
        return w[0].astype(BF)

    def fetch(k, low, high, *needed):
        return lax.ppermute(
            after(piece_of(k, low, high), *needed), "dp", [(i, i ^ k) for i in range(Z)]
        )

    gate_far = fetch(2, 0, 1, w_proj)
    up_far = fetch(2, 1, 2, gate_far)

    cosine, sine = rope_tables(L, HD)
    score_scale = HD ** (-0.5)
    documents = doc_ids[0]
    position = jnp.arange(L)
    allowed = (
        (position[None, :] <= position[:, None]) & (documents[None, :] == documents[:, None])
    )[None]
    turned = (lax.axis_index("expert") * share + jnp.arange(share)) < 2 * D // HD
    turned = turned[None, None, :, None].astype(F32)
    cos_mine = cosine[None, :, None, :] * turned + (1.0 - turned)
    sin_mine = sine[None, :, None, :] * turned
    projected = mm(unit_all, w_proj).reshape(E, L, share, HD)
    half = HD // 2
    crossed = jnp.concatenate([-projected[..., half:], projected[..., :half]], -1)
    heads_in = (projected * cos_mine + crossed * sin_mine).astype(BF).reshape(E, L, wide)
    hot_own = jnp.sum(
        (routes[:, :, None] == jnp.arange(experts, dtype=jnp.int32)).astype(F32), 1
    )
    hot_wide = jnp.pad(hot_own, ((0, 0), (0, 128 - experts))).astype(BF)
    grad_hot = jnp.concatenate([cotangent, hot_wide], 1)
    heads_in = lax.all_to_all(heads_in, "expert", split_axis=0, concat_axis=0, tiled=True)
    grad_hot = gather_z(after(grad_hot, w_proj), (heads_in,))
    grad_in = grad_hot[:, :, :D]
    hot = grad_hot[:, :, D : D + experts].astype(F32)

    doc_row = doc_ids.astype(jnp.int32)
    doc_col = doc_row.reshape(L, 1)
    heads_out = attend(after(heads_in, gate_far), doc_row, doc_col)
    gain_row = gain_second[None, :]
    middle, inner, attn_square = project_out(
        heads_out, tokens, packed, gain_row
    )

    sw = after(shared_weight, inner).astype(BF)
    sw = [lax.dynamic_slice(sw, (0, 0, (zi ^ k) * FS), (3, R, FS)) for k in range(Z)]
    sw = jnp.stack(swap_z(sw), 1)
    sw = lax.all_gather(sw, "expert", axis=2, tiled=False)
    full = jnp.zeros((3, Z, E, R, FS), BF)
    for k in range(Z):
        full = lax.dynamic_update_slice(full, sw[:, k][:, None], (0, zi ^ k, 0, 0, 0))
    shared_w = full.reshape(3, D, FS)

    before = (position[None, :] < position[:, None]).astype(BF)
    rank = jnp.einsum("tu,sux->stx", before, hot.astype(BF), preferred_element_type=F32)
    first = zi // parts
    mine = jnp.arange(E) * local + first
    pick = (jnp.arange(experts)[:, None] == mine[None, :]).astype(F32)
    hot_mine = jnp.einsum("stx,xe->est", hot, pick)
    rank_mine = jnp.einsum("stx,xe->est", rank, pick, precision=lax.Precision.HIGHEST)
    place = (
        (rank_mine[:, :, None, :] == jnp.arange(cap, dtype=F32)[None, None, :, None])
        & (hot_mine[:, :, None, :] > 0.5)
    ).astype(BF)

    def dispatch(x):
        rows = jnp.einsum("esct,std->escd", place, x, preferred_element_type=F32).astype(BF)
        return lax.all_to_all(rows, "expert", split_axis=0, concat_axis=0, tiled=True).reshape(
            E * Z * cap, x.shape[-1]
        )

    def gates_of(logits, hot_in):
        chosen = jnp.where(hot_in > 0.5, logits, masked_score)
        top = jnp.max(chosen, -1, keepdims=True)
        parts_in = jnp.where(hot_in > 0.5, jnp.exp(chosen - top), 0.0)
        return parts_in / jnp.maximum(jnp.sum(parts_in, -1, keepdims=True), 0.5)

    grad_rows_hot = dispatch(grad_hot)

    inner_z = gather_z(after(inner, grad_hot, up_far))
    near = fetch(1, 0, 2, inner_z)
    front = [[piece_of(0, 0, 1), near[:1], gate_far], [piece_of(0, 1, 2), near[1:], up_far]]
    last = up_far
    for k in range(3, Z):
        for m in range(2):
            last = fetch(k, m, m + 1, last)
            front[m].append(last)
    rows = dispatch(after(inner_z, grad_rows_hot, *[f[3] for f in front[:1] if Z > 3]))
    down = [piece_of(0, 2, 3)] + [fetch(k, 2, 3, last) for k in range(1, Z)]

    place_of = jnp.stack([zi, ei * local + first]).astype(jnp.int32)
    router_wide = packed[:, D:]
    eg, eu, gated, gate_col = expert_front(place_of, rows, grad_rows_hot, router_wide, front[0] + front[1])
    down_grad = weight_grads(grad_rows_hot, [gated], D)

    def send_grads(g, last):
        got = [None] * Z
        for k in [0] + list(range(2, Z)) + [1]:
            piece = lax.dynamic_slice(g, (0, (zi ^ k) * deep, 0), (g.shape[0], deep, FP))
            if k > 0:
                piece = after(piece, last) if last is not None else piece
                piece = lax.ppermute(piece, "dp", [(i, i ^ k) for i in range(Z)])
                last = piece if k != 1 else last
            got[k] = piece
        return got, last

    down_got, last_down = send_grads(down_grad, None)
    rows_grad, routed_rows, eg_grad, eu_grad, gate_grad = expert_back(
        place_of, grad_rows_hot, eg, eu, after(gated, down_grad), gate_col, front[0] + front[1], down,
        Z * cap,
    )

    gate_grad_back = lax.all_to_all(
        gate_grad, "expert", split_axis=0, concat_axis=0, tiled=True
    )[:, 0].reshape(E, Z, cap)
    front_grad = weight_grads(
        after(rows, gate_grad_back, down_got[2]), [eg_grad, eu_grad], D
    )
    front_got, _ = send_grads(front_grad, last_down)

    flat_inner = after(inner_z, front_grad).reshape(Z * L, D)
    flat_grad = grad_in.reshape(Z * L, D)
    sg = mm(flat_inner, shared_w[0])
    su = mm(flat_inner, shared_w[1])
    ssig = jax.nn.sigmoid(sg)
    ssilu = sg * ssig
    shared_hidden = (ssilu * su).astype(BF)
    shared_out = mm_nt(shared_hidden, shared_w[2])
    shared_hidden_grad = mm(flat_grad, shared_w[2])
    sg_grad = (shared_hidden_grad * su * ssig * (1.0 + sg * (1.0 - ssig))).astype(BF)
    su_grad = (shared_hidden_grad * ssilu).astype(BF)
    shared_back = mm_nt(sg_grad, shared_w[0]) + mm_nt(su_grad, shared_w[1])
    shared_grads = jnp.stack(
        [mm_tn(flat_inner, sg_grad), mm_tn(flat_inner, su_grad), mm_tn(flat_grad, shared_hidden)]
    ).astype(BF)

    def collect(rows_in, add):
        back = lax.all_to_all(
            rows_in.reshape(E, Z, cap, D), "expert", split_axis=0, concat_axis=0, tiled=True
        )
        total = jnp.einsum("esct,escd->std", place, back, preferred_element_type=F32) + add
        return back, total.astype(BF)

    gate_grad_mine = jnp.sum(place.astype(F32) * gate_grad_back[:, :, :, None], 2)
    gate_grad_z = jnp.einsum(
        "est,xe->stx", gate_grad_mine, pick, precision=lax.Precision.HIGHEST
    ).reshape(Z * L, experts)
    gates_z = gates_of(mm(flat_inner, router_w), hot.reshape(Z * L, experts))
    logit_grad = gates_z * (gate_grad_z - jnp.sum(gates_z * gate_grad_z, -1, keepdims=True))
    router_grad = mm_tn(flat_inner.astype(F32), logit_grad)
    router_back = mm_nt(logit_grad, router_w.astype(F32))

    rows_back, inner_grad = collect(rows_grad, (shared_back + router_back).reshape(Z, L, D))
    inner_grad = reduce_z(after(inner_grad, *down_got[2:]))
    routed_back, branch = collect(after(routed_rows, rows_back), shared_out.reshape(Z, L, D))

    def reduce_rows(x):
        x = jnp.swapaxes(x.reshape(Z, E, R, x.shape[1]), 0, 1).reshape(D, x.shape[1])
        x = lax.psum_scatter(x, "expert", scatter_dimension=0, tiled=True)
        x = x.reshape(Z, R, x.shape[1])
        return jnp.concatenate([lax.dynamic_slice_in_dim(x, zi ^ o, 1, 0) for o in offs], 0)

    middle_grad, attn_grad, second_gain_grad, proj_grad = attend_back(
        after(inner_grad, front_got[2]), cotangent, middle, packed, gain_row, heads_in, doc_row, doc_col, cosine, sine
    )
    output_grad = mm_tn(heads_out, attn_grad)
    pad = jnp.zeros((D, 128 - experts - 1), F32)
    small_all = jnp.concatenate(
        [output_grad, router_grad, second_gain_grad.T, pad], 1
    ).astype(BF)
    small_own = reduce_rows(small_all)

    proj_grad = lax.all_to_all(after(proj_grad, routed_back), "expert", split_axis=0, concat_axis=0, tiled=True)
    proj_grad = proj_grad.reshape(E * L, wide)
    proj_w_grad = mm_tn(unit_all, proj_grad).astype(BF).reshape(Z * E, R, wide)
    proj_w_local = proj_w_grad
    small_own = reduce_z(after(small_own, proj_w_local))
    proj_w_grad = lax.all_to_all(proj_w_grad, ALL, split_axis=0, concat_axis=0, tiled=True)
    proj_sum = jnp.sum(proj_w_grad.reshape(Z, E, R, wide).astype(F32), 0)
    proj_sum = jnp.swapaxes(proj_sum, 0, 1).reshape(R, E * wide)[:, : 3 * D]
    proj_sum = jnp.swapaxes(proj_sum.reshape(R, 3, D), 0, 1)

    back = mm_nt(proj_grad, w_proj).astype(BF)
    back_local = back
    scaled_first = lax.psum_scatter(back, "expert", scatter_dimension=0, tiled=True).astype(F32)
    input_grad = middle_grad + inv_first * (
        scaled_first - unit_first * jnp.mean(scaled_first * unit_first, -1, keepdims=True)
    )

    branch = reduce_z(after(branch, back_local))
    layer_out = (middle + branch).astype(BF)
    first_mask = jnp.concatenate([jnp.ones((1,), bool), documents[1:] != documents[:-1]])
    kept_mask = 1.0 - first_mask.astype(F32)
    kept_total = jnp.sum(kept_mask) * D
    attn_rms = jnp.sqrt(jnp.sum(kept_mask * attn_square[:, 0]) / kept_total)
    branch_rms = jnp.sqrt(jnp.sum(kept_mask[:, None] * branch * branch) / kept_total)
    sublayer_rms = jnp.stack([attn_rms, branch_rms])[None, :]

    first_gain_grad = jnp.sum(proj_sum * attn_weight[:3].astype(BF).astype(F32), (0, 2))
    attn_sum = jnp.concatenate(
        [proj_sum * gain_low[0][None, :, None], small_own[None, :, :D]], 0
    )
    router_sum = small_own[:, D : D + experts]
    gain_sum = jnp.stack([first_gain_grad, small_own[:, D + experts]])

    owned = (expert_weight, expert_momentum, expert_average)
    expert_new = ()
    expert_sum = jnp.zeros((local, 3, deep, FF), BF)
    for m, gots in ((2, down_got), (0, front_got)):
        for k in [0] + list(range(2, Z)) + [1]:
            there = zi ^ k
            got = gots[k]
            if parts == 1:
                if k > 0:
                    got = after(got, proj_w_local, branch)
                expert_new = update_part(owned, expert_new, got, m, there)
            else:
                expert_sum = lax.dynamic_update_slice(
                    expert_sum, got[None], (there // parts, m, 0, (there % parts) * FP)
                )
    if parts > 1:
        expert_new = update(*owned, expert_sum.astype(F32), rate_expert)

    sgr = shared_grads.reshape(3, Z, E, R, FS).transpose(2, 1, 0, 3, 4).reshape(E * Z * 3 * R, FS)
    sgr = lax.psum_scatter(sgr, "expert", scatter_dimension=0, tiled=True)
    sgr = after(sgr.reshape(Z, 3, R, FS), inner_grad)
    got = swap_z(
        [lax.dynamic_index_in_dim(sgr, zi ^ k, 0, keepdims=False) for k in range(Z)]
    )
    shared_sum = jnp.zeros((3, R, Z * FS), BF)
    for k in range(Z):
        shared_sum = lax.dynamic_update_slice(shared_sum, got[k], (0, 0, (zi ^ k) * FS))
    shared_sum = shared_sum.astype(F32)

    attn_rates = jnp.array([rate_attn, rate_attn, rate_attn, rate_output], F32).reshape(4, 1, 1)
    return (
        layer_out,
        input_grad,
        *update(attn_weight, attn_momentum, attn_average, attn_sum, attn_rates),
        *update(shared_weight, shared_momentum, shared_average, shared_sum, rate_shared),
        *update(router_weight, router_momentum, router_average, router_sum, rate_router),
        *update(gain_weight, gain_momentum, gain_average, gain_sum, rate_gain),
        *expert_new,
        sublayer_rms,
    )


def solution(mesh):
    rows = P(ALL, None)
    middle = P(None, ALL, None)
    gains = P(None, ALL)
    routed = P("expert", None, "dp", None)
    weights = (middle,) * 6 + (rows,) * 3 + (gains,) * 3 + (routed,) * 3
    return jax.shard_map(
        body,
        mesh=mesh,
        in_specs=(rows,) * 4 + weights,
        out_specs=(rows,) * 2 + weights + (rows,),
        check_vma=False,
    )
```

```python
import functools
import math

import jax
import jax.numpy as jnp
from jax import lax
from jax.experimental import pallas as pl
from jax.experimental.pallas import tpu as pltpu
from jax.sharding import PartitionSpec as P

HEADS = 10
HD = 128
TOPK = 7
STEP = 3
BF = jnp.bfloat16
F32 = jnp.float32

epsilon = 1e-06
momentum_decay = 0.9
masked_score = -1e30
rate_attn = 5e-05
rate_output = 0.0002
rate_shared = 0.0001
rate_router = 3e-05
rate_gain = 0.002
rate_expert = 0.0015
ALL = ("dp", "expert")


def rope_tables(length, size):
    half = size // 2
    freq = jnp.exp(jnp.arange(half, dtype=F32) * (-2.0 * math.log(10000.0) / size))
    angle = jnp.arange(length, dtype=F32)[:, None] * freq[None, :]
    cosine = jnp.concatenate([jnp.cos(angle), jnp.cos(angle)], -1)
    sine = jnp.concatenate([jnp.sin(angle), jnp.sin(angle)], -1)
    return (cosine, sine)


def update(weight, moment, average, grad, rate):
    moment_new = momentum_decay * moment + grad
    weight_new = weight - rate * (grad + momentum_decay * moment_new)
    average_new = average + (weight_new - average) / (STEP + 1.0)
    return (weight_new, moment_new, average_new)


def mm(a, b):
    return jnp.dot(a, b, preferred_element_type=F32)


def mm_nt(a, b):
    return lax.dot_general(a, b, (((1,), (1,)), ((), ())), preferred_element_type=F32)


def mm_tn(a, b):
    return lax.dot_general(a, b, (((0,), (0,)), ((), ())), preferred_element_type=F32)


def attend_probs(heads_ref, doc_row_ref, doc_col_ref, block):
    share = heads_ref.shape[2] // HD

    def head(b):
        return heads_ref[b // share, :, (b % share) * HD : (b % share + 1) * HD]

    length = heads_ref.shape[1]
    row = lax.broadcasted_iota(jnp.int32, (length, length), 0)
    col = lax.broadcasted_iota(jnp.int32, (length, length), 1)
    allowed = (col <= row) & (doc_row_ref[...] == doc_col_ref[...])
    query, key = head(block), head(HEADS + block)
    scores = jnp.where(allowed, mm_nt(query, key) * HD ** (-0.5), masked_score)
    exponent = jnp.exp(scores - jnp.max(scores, -1, keepdims=True))
    probs = exponent / jnp.sum(exponent, -1, keepdims=True)
    return query, key, head(2 * HEADS + block), probs


def attend_kernel(heads_ref, doc_row_ref, doc_col_ref, out_ref):
    for h in range(HEADS):
        _, _, value, probs = attend_probs(heads_ref, doc_row_ref, doc_col_ref, h)
        out_ref[:, h * HD : (h + 1) * HD] = mm(probs.astype(BF), value).astype(BF)


def attend(heads, doc_row, doc_col):
    return pl.pallas_call(
        attend_kernel,
        out_shape=jax.ShapeDtypeStruct((heads.shape[1], HEADS * HD), BF),
        compiler_params=pltpu.CompilerParams(vmem_limit_bytes=24 << 20),
        name="attend",
    )(heads, doc_row, doc_col)


def out_kernel(heads_ref, tokens_ref, w_ref, gain_ref, middle_ref, inner_ref, square_ref):
    attn_out = mm(heads_ref[...], w_ref[...])
    middle = tokens_ref[...].astype(F32) + attn_out
    scale = lax.rsqrt(jnp.mean(middle * middle, -1, keepdims=True) + epsilon)
    middle_ref[...] = middle
    inner_ref[...] = (middle * scale * gain_ref[...]).astype(BF)
    square = jnp.sum(attn_out * attn_out, -1, keepdims=True)
    square_ref[...] = jnp.broadcast_to(square, square_ref.shape)


def project_out(heads_out, tokens, packed, gain):
    length, width = tokens.shape
    return pl.pallas_call(
        out_kernel,
        grid=(1,),
        in_specs=[
            pl.BlockSpec((length, width), lambda i: (0, 0)),
            pl.BlockSpec((length, width), lambda i: (0, 0)),
            pl.BlockSpec((width, width), lambda i: (0, 0)),
            pl.BlockSpec((1, width), lambda i: (0, 0)),
        ],
        out_specs=[
            pl.BlockSpec((length, width), lambda i: (0, 0)),
            pl.BlockSpec((length, width), lambda i: (0, 0)),
            pl.BlockSpec((length, 128), lambda i: (0, 0)),
        ],
        out_shape=[
            jax.ShapeDtypeStruct((length, width), F32),
            jax.ShapeDtypeStruct((length, width), BF),
            jax.ShapeDtypeStruct((length, 128), F32),
        ],
        compiler_params=pltpu.CompilerParams(vmem_limit_bytes=24 << 20),
        name="project_out",
    )(heads_out, tokens, packed, gain)


def attend_back_kernel(
    ig_ref, g_ref, middle_ref, w_ref, gain_ref, heads_ref, doc_row_ref, doc_col_ref,
    cos_ref, sin_ref, mg_ref, ag_ref, gain_out, out_ref, hg_ref
):
    grad = ig_ref[...]
    middle = middle_ref[...]
    scale = lax.rsqrt(jnp.mean(middle * middle, -1, keepdims=True) + epsilon)
    unit = middle * scale
    scaled = grad * gain_ref[...]
    gain_out[...] = jnp.sum(grad * unit, 0, keepdims=True)
    middle_grad = g_ref[...].astype(F32) + scale * (
        scaled - unit * jnp.mean(scaled * unit, -1, keepdims=True)
    )
    mg_ref[...] = middle_grad
    attn_grad = middle_grad.astype(BF)
    ag_ref[...] = attn_grad
    hg_ref[...] = mm_nt(attn_grad, w_ref[...]).astype(BF)
    share = heads_ref.shape[2] // HD

    def put(b, value):
        out_ref[b // share, :, (b % share) * HD : (b % share + 1) * HD] = value

    lane = lax.broadcasted_iota(jnp.int32, cos_ref.shape, 1)
    sign_sin = jnp.where(lane < HD // 2, -sin_ref[...], sin_ref[...])

    def rotate_back(z):
        return (z * cos_ref[...] + pltpu.roll(z * sign_sin, HD // 2, 1)).astype(BF)

    for h in range(HEADS):
        query, key, value, probs = attend_probs(heads_ref, doc_row_ref, doc_col_ref, h)
        out_grad = hg_ref[:, h * HD : (h + 1) * HD]
        prob_grad = mm_nt(out_grad, value)
        score_grad = (
            probs * (prob_grad - jnp.sum(probs * prob_grad, -1, keepdims=True))
        ).astype(BF)
        put(h, rotate_back(mm(score_grad, key) * HD ** (-0.5)))
        put(HEADS + h, rotate_back(mm_tn(score_grad, query) * HD ** (-0.5)))
        put(2 * HEADS + h, mm_tn(probs.astype(BF), out_grad).astype(BF))
    for b in range(3 * HEADS, heads_ref.shape[0] * share):
        put(b, jnp.zeros((heads_ref.shape[1], HD), BF))


def attend_back(grad, cotangent, middle, packed, gain, heads, doc_row, doc_col, cosine, sine):
    length, width = middle.shape
    whole = pl.BlockSpec((length, width), lambda i: (0, 0))
    table = pl.BlockSpec((length, HD), lambda i: (0, 0))
    row = pl.BlockSpec((1, width), lambda i: (0, 0))
    blocks = pl.BlockSpec(heads.shape, lambda i: (0, 0, 0))
    return pl.pallas_call(
        attend_back_kernel,
        grid=(1,),
        in_specs=[
            whole,
            whole,
            whole,
            pl.BlockSpec((width, width), lambda i: (0, 0)),
            row,
            blocks,
            pl.BlockSpec((1, length), lambda i: (0, 0)),
            pl.BlockSpec((length, 1), lambda i: (0, 0)),
            table,
            table,
        ],
        out_specs=[whole, whole, row, blocks],
        out_shape=[
            jax.ShapeDtypeStruct((length, width), F32),
            jax.ShapeDtypeStruct((length, width), BF),
            jax.ShapeDtypeStruct((1, width), F32),
            jax.ShapeDtypeStruct(heads.shape, BF),
        ],
        scratch_shapes=[pltpu.VMEM((length, width), BF)],
        compiler_params=pltpu.CompilerParams(vmem_limit_bytes=32 << 20),
        name="attend_back",
    )(grad, cotangent, middle, packed, gain, heads, doc_row, doc_col, cosine, sine)


def load_pieces(zi, pieces, dest, sem):
    depth = pieces[0].shape[1]
    copies = [
        pltpu.make_async_copy(
            piece,
            dest.at[:, pl.ds(pl.multiple_of((zi ^ k) * depth, 16), depth)],
            sem.at[k],
        )
        for k, piece in enumerate(pieces)
    ]
    for copy in copies:
        copy.start()
    for copy in copies:
        copy.wait()


def front_kernel(count, place_ref, x_ref, hot_ref, router_ref, *rest):
    pieces = rest[:count]
    eg_ref, eu_ref, gated_ref, gate_ref, w_ref, sem = rest[count:]

    @pl.when(pl.program_id(0) == 0)
    def _():
        half = count // 2
        load_pieces(place_ref[0], pieces[:half], w_ref.at[pl.ds(0, 1)], sem)
        load_pieces(place_ref[0], pieces[half:], w_ref.at[pl.ds(1, 1)], sem)

    x = x_ref[...]
    hot = hot_ref[...].astype(F32) > 0.5
    chosen = jnp.where(hot, mm(x, router_ref[...]), masked_score)
    top = jnp.max(chosen, -1, keepdims=True)
    exponent = jnp.where(hot, jnp.exp(chosen - top), 0.0)
    lane = lax.broadcasted_iota(jnp.int32, exponent.shape, 1)
    own = jnp.sum(jnp.where(lane == place_ref[1], exponent, 0.0), -1, keepdims=True)
    gate = own / jnp.maximum(jnp.sum(exponent, -1, keepdims=True), 0.5)
    eg = mm(x, w_ref[0])
    eu = mm(x, w_ref[1])
    eg_ref[...] = eg
    eu_ref[...] = eu
    gated_ref[...] = (gate * (eg * jax.nn.sigmoid(eg) * eu)).astype(BF)
    gate_ref[...] = jnp.broadcast_to(gate, gate_ref.shape)


def tile_of(count):
    return next(t for t in (256, 192, 128, 64, 48, 16, 8) if count % t == 0)


def expert_front(place, rows, grads_hot, router, pieces):
    count, width = rows.shape
    hidden = pieces[0].shape[2]
    tile = tile_of(count)
    extra = grads_hot.shape[1] - width
    flops = 4 * count * width * hidden
    return pl.pallas_call(
        functools.partial(front_kernel, len(pieces)),
        grid_spec=pltpu.PrefetchScalarGridSpec(
            num_scalar_prefetch=1,
            grid=(count // tile,),
            in_specs=[
                pl.BlockSpec((tile, width), lambda i, p: (i, 0)),
                pl.BlockSpec((tile, extra), lambda i, p: (i, width // extra)),
                pl.BlockSpec((width, extra), lambda i, p: (0, 0)),
            ]
            + [pl.BlockSpec(memory_space=pl.ANY)] * len(pieces),
            out_specs=[pl.BlockSpec((tile, hidden), lambda i, p: (i, 0))] * 3
            + [pl.BlockSpec((tile, 128), lambda i, p: (i, 0))],
            scratch_shapes=[
                pltpu.VMEM((2, width, hidden), BF),
                pltpu.SemaphoreType.DMA((len(pieces),)),
            ],
        ),
        out_shape=[
            jax.ShapeDtypeStruct((count, hidden), F32),
            jax.ShapeDtypeStruct((count, hidden), F32),
            jax.ShapeDtypeStruct((count, hidden), BF),
            jax.ShapeDtypeStruct((count, 128), F32),
        ],
        cost_estimate=pl.CostEstimate(
            flops=flops, bytes_accessed=12 * count * hidden, transcendentals=0
        ),
        compiler_params=pltpu.CompilerParams(vmem_limit_bytes=40 << 20),
        name="expert_front",
    )(place, rows, grads_hot, router, *pieces)


def back_kernel(count, place_ref, g_ref, eg_ref, eu_ref, gated_ref, gate_ref, *rest):
    gate_w, up_w, down = rest[:count], rest[count : 2 * count], rest[2 * count : 3 * count]
    rows_ref, routed_ref, egg_ref, eug_ref, gg_ref, w_ref, wd_ref, sem = rest[3 * count :]

    @pl.when(pl.program_id(0) == 0)
    def _():
        load_pieces(place_ref[0], down, wd_ref, sem)
        load_pieces(place_ref[0], gate_w, w_ref.at[pl.ds(0, 1)], sem)
        load_pieces(place_ref[0], up_w, w_ref.at[pl.ds(1, 1)], sem)

    eg = eg_ref[...]
    eu = eu_ref[...]
    sig = jax.nn.sigmoid(eg)
    silu = eg * sig
    plain = mm(g_ref[...], wd_ref[0])
    gate_grad = jnp.sum(silu * eu * plain, -1, keepdims=True)
    count = gg_ref.shape[2]
    for i in range(gg_ref.shape[0]):
        part = gate_grad[i * count : (i + 1) * count]
        gg_ref[i] = jnp.broadcast_to(part, (count, 128)).T[:8]
    grad = gate_ref[:, :1] * plain
    eg_grad = (grad * eu * sig * (1.0 + eg * (1.0 - sig))).astype(BF)
    eu_grad = (grad * silu).astype(BF)
    egg_ref[...] = eg_grad
    eug_ref[...] = eu_grad
    rows_ref[...] = (mm_nt(eg_grad, w_ref[0]) + mm_nt(eu_grad, w_ref[1])).astype(BF)
    routed_ref[...] = mm_nt(gated_ref[...], wd_ref[0]).astype(BF)


def expert_back(place, grads_hot, eg, eu, gated, gate, front, down, group):
    count, hidden = eg.shape
    deep = front[0].shape[1]
    width = deep * len(down)
    tile = 2 * group if count % (2 * group) == 0 else group
    wide = pl.BlockSpec((tile, width), lambda i, p: (i, 0))
    thin = pl.BlockSpec((tile, hidden), lambda i, p: (i, 0))
    lanes = pl.BlockSpec((tile, 128), lambda i, p: (i, 0))
    return pl.pallas_call(
        functools.partial(back_kernel, len(down)),
        grid_spec=pltpu.PrefetchScalarGridSpec(
            num_scalar_prefetch=1,
            grid=(count // tile,),
            in_specs=[wide, thin, thin, thin, lanes]
            + [pl.BlockSpec(memory_space=pl.ANY)] * (3 * len(down)),
            out_specs=[wide, wide, thin, thin, pl.BlockSpec((tile // group, 8, group), lambda i, p: (i, 0, 0))],
            scratch_shapes=[
                pltpu.VMEM((2, width, hidden), BF),
                pltpu.VMEM((1, width, hidden), BF),
                pltpu.SemaphoreType.DMA((len(down),)),
            ],
        ),
        out_shape=[
            jax.ShapeDtypeStruct((count, width), BF),
            jax.ShapeDtypeStruct((count, width), BF),
            jax.ShapeDtypeStruct((count, hidden), BF),
            jax.ShapeDtypeStruct((count, hidden), BF),
            jax.ShapeDtypeStruct((count // group, 8, group), F32),
        ],
        cost_estimate=pl.CostEstimate(
            flops=8 * count * width * hidden,
            bytes_accessed=16 * count * hidden,
            transcendentals=0,
        ),
        compiler_params=pltpu.CompilerParams(vmem_limit_bytes=48 << 20),
        name="expert_back",
    )(place, grads_hot, eg, eu, gated, gate, *front, *down)


def weight_grads(x, ys, width):
    count = x.shape[0]
    hidden = ys[0].shape[1]
    tile = 256
    return pl.pallas_call(
        grads_body(len(ys)),
        grid=(width // tile,),
        in_specs=[pl.BlockSpec((count, tile), lambda i: (0, i))]
        + [pl.BlockSpec((count, hidden), lambda i: (0, 0))] * len(ys),
        out_specs=pl.BlockSpec((len(ys), tile, hidden), lambda i: (0, i, 0)),
        out_shape=jax.ShapeDtypeStruct((len(ys), width, hidden), BF),
        cost_estimate=pl.CostEstimate(
            flops=2 * len(ys) * count * width * hidden,
            bytes_accessed=2 * count * (width + hidden),
            transcendentals=0,
        ),
        compiler_params=pltpu.CompilerParams(vmem_limit_bytes=40 << 20),
        name="weight_grads",
    )(x, *ys)


def grads_body(many):
    def kernel(x_ref, *rest):
        x = x_ref[...]
        for i in range(many):
            rest[many][i] = mm_tn(x, rest[i][...]).astype(BF)

    return kernel


def update_kernel(place_ref, w_ref, m_ref, a_ref, g_ref, *rest):
    w_out, m_out, a_out = rest[-3:]
    new = update(w_ref[0, 0], m_ref[0, 0], a_ref[0, 0], g_ref[0].astype(F32), rate_expert)
    w_out[0, 0], m_out[0, 0], a_out[0, 0] = new


def update_part(owned, so_far, grad, low, place):
    count, deep, width = grad.shape
    tile = deep // 2
    state = pl.BlockSpec((1, 1, tile, width), lambda m, t, p: (p[0], low + m, t, 0))
    moved = 6 * 4 * grad.size + 2 * grad.size
    return pl.pallas_call(
        update_kernel,
        grid_spec=pltpu.PrefetchScalarGridSpec(
            num_scalar_prefetch=1,
            grid=(count, deep // tile),
            in_specs=[state] * 3
            + [pl.BlockSpec((1, tile, width), lambda m, t, p: (m, t, 0))]
            + [pl.BlockSpec(memory_space=pl.ANY)] * len(so_far),
            out_specs=[state] * 3,
        ),
        out_shape=[jax.ShapeDtypeStruct(x.shape, x.dtype) for x in owned],
        input_output_aliases={5 + i: i for i in range(len(so_far))},
        cost_estimate=pl.CostEstimate(
            flops=8 * grad.size, bytes_accessed=moved, transcendentals=0
        ),
        compiler_params=pltpu.CompilerParams(vmem_limit_bytes=60 << 20),
        name="update_part",
    )(jnp.reshape(place, (1,)).astype(jnp.int32), *owned, grad, *so_far)


def body(
    tokens,
    cotangent,
    routes,
    doc_ids,
    attn_weight,
    attn_momentum,
    attn_average,
    shared_weight,
    shared_momentum,
    shared_average,
    router_weight,
    router_momentum,
    router_average,
    gain_weight,
    gain_momentum,
    gain_average,
    expert_weight,
    expert_momentum,
    expert_average,
):
    Z = lax.axis_size("dp")
    E = lax.axis_size("expert")
    L, D = tokens.shape
    rows_own = attn_weight.shape[1]
    local, _, deep, FF = expert_weight.shape
    experts = router_weight.shape[1]
    parts = Z // local
    FP = FF // parts
    FS = shared_weight.shape[2] // Z
    cap = min(L, (L * TOPK * 3 // (2 * experts) + 7) // 8 * 8)
    zi = lax.axis_index("dp")

    def swap_z(pieces):
        out = [pieces[0]]
        for k in range(1, Z):
            out.append(lax.ppermute(pieces[k], "dp", [(i, i ^ k) for i in range(Z)]))
        return out

    strides = [1 << b for b in range(Z.bit_length() - 1)][::-1]
    offs = [0]
    for stride in strides:
        offs = offs + [o ^ stride for o in offs]

    def gather_z(x, then=()):
        held = x[None]
        for step, stride in enumerate(strides):
            if step > 0 and then:
                held = after(held, *then)
            got = lax.ppermute(held, "dp", [(i, i ^ stride) for i in range(Z)])
            held = jnp.concatenate([held, got], 0)
        return held

    def reduce_z(x):
        for stride in strides[::-1]:
            keep, send = jnp.split(x, 2, 0)
            got = lax.ppermute(send, "dp", [(i, i ^ stride) for i in range(Z)])
            total = keep.astype(F32) + got.astype(F32)
            x = total.astype(BF)
        return total[0]

    R = rows_own
    ei = lax.axis_index("expert")

    def after(x, *needed):
        return lax.optimization_barrier((x,) + needed)[0]

    blocks = 3 * D // HD
    share = -(-blocks // E)
    wide = share * HD
    gain_low = gain_weight.astype(BF).astype(F32)
    folded = (attn_weight[:3].astype(BF).astype(F32) * gain_low[0][None, :, None]).astype(BF)
    folded = jnp.swapaxes(folded, 0, 1).reshape(R, 3 * D)
    folded = jnp.pad(folded, ((0, 0), (0, E * wide - 3 * D)))
    folded = jnp.swapaxes(folded.reshape(R, E, wide), 0, 1)
    folded = jnp.broadcast_to(folded[None], (Z, E, R, wide)).reshape(Z * E, R, wide)
    w_proj = lax.all_to_all(folded, ALL, split_axis=0, concat_axis=0, tiled=True)
    w_proj = w_proj.reshape(D, wide)

    inputs = tokens.astype(F32)
    inv_first = lax.rsqrt(jnp.mean(inputs * inputs, -1, keepdims=True) + epsilon)
    unit_first = inputs * inv_first
    unit_all = lax.all_gather(unit_first.astype(BF), "expert", axis=0, tiled=True)

    extra = jnp.concatenate([router_weight, gain_weight[1:].T], 1).astype(BF)
    extra = jnp.pad(extra, ((0, 0), (0, 128 - extra.shape[1])))
    packed = jnp.concatenate([attn_weight[3].astype(BF), extra], 1)
    packed = lax.all_gather(gather_z(packed), "expert", axis=0, tiled=False)
    full = jnp.zeros((Z, E, R, D + 128), BF)
    for k, o in enumerate(offs):
        full = lax.dynamic_update_slice(full, packed[:, k][None], (zi ^ o, 0, 0, 0))
    packed = full.reshape(D, D + 128)
    w_o = packed[:, :D]
    router_w = packed[:, D : D + experts]
    gain_second = packed[:, D + experts].astype(F32)

    def piece_of(k, low, high):
        there = zi ^ k
        w = lax.dynamic_slice(
            expert_weight,
            (there // parts, low, 0, (there % parts) * FP),
            (1, high - low, deep, FP),
        )
        return w[0].astype(BF)

    def fetch(k, low, high, *needed):
        return lax.ppermute(
            after(piece_of(k, low, high), *needed), "dp", [(i, i ^ k) for i in range(Z)]
        )

    gate_far = fetch(2, 0, 1, w_proj)
    up_far = fetch(2, 1, 2, gate_far)

    cosine, sine = rope_tables(L, HD)
    score_scale = HD ** (-0.5)
    documents = doc_ids[0]
    position = jnp.arange(L)
    allowed = (
        (position[None, :] <= position[:, None]) & (documents[None, :] == documents[:, None])
    )[None]
    turned = (lax.axis_index("expert") * share + jnp.arange(share)) < 2 * D // HD
    turned = turned[None, None, :, None].astype(F32)
    cos_mine = cosine[None, :, None, :] * turned + (1.0 - turned)
    sin_mine = sine[None, :, None, :] * turned
    projected = mm(unit_all, w_proj).reshape(E, L, share, HD)
    half = HD // 2
    crossed = jnp.concatenate([-projected[..., half:], projected[..., :half]], -1)
    heads_in = (projected * cos_mine + crossed * sin_mine).astype(BF).reshape(E, L, wide)
    hot_own = jnp.sum(
        (routes[:, :, None] == jnp.arange(experts, dtype=jnp.int32)).astype(F32), 1
    )
    hot_wide = jnp.pad(hot_own, ((0, 0), (0, 128 - experts))).astype(BF)
    grad_hot = jnp.concatenate([cotangent, hot_wide], 1)
    heads_in = lax.all_to_all(heads_in, "expert", split_axis=0, concat_axis=0, tiled=True)
    grad_hot = gather_z(after(grad_hot, w_proj), (heads_in,))
    grad_in = grad_hot[:, :, :D]
    hot = grad_hot[:, :, D : D + experts].astype(F32)

    doc_row = doc_ids.astype(jnp.int32)
    doc_col = doc_row.reshape(L, 1)
    heads_out = attend(after(heads_in, gate_far), doc_row, doc_col)
    gain_row = gain_second[None, :]
    middle, inner, attn_square = project_out(
        heads_out, tokens, packed, gain_row
    )

    sw = after(shared_weight, inner).astype(BF)
    sw = [lax.dynamic_slice(sw, (0, 0, (zi ^ k) * FS), (3, R, FS)) for k in range(Z)]
    sw = jnp.stack(swap_z(sw), 1)
    sw = lax.all_gather(sw, "expert", axis=2, tiled=False)
    full = jnp.zeros((3, Z, E, R, FS), BF)
    for k in range(Z):
        full = lax.dynamic_update_slice(full, sw[:, k][:, None], (0, zi ^ k, 0, 0, 0))
    shared_w = full.reshape(3, D, FS)

    before = (position[None, :] < position[:, None]).astype(BF)
    rank = jnp.einsum("tu,sux->stx", before, hot.astype(BF), preferred_element_type=F32)
    first = zi // parts
    mine = jnp.arange(E) * local + first
    pick = (jnp.arange(experts)[:, None] == mine[None, :]).astype(F32)
    hot_mine = jnp.einsum("stx,xe->est", hot, pick)
    rank_mine = jnp.einsum("stx,xe->est", rank, pick, precision=lax.Precision.HIGHEST)
    place = (
        (rank_mine[:, :, None, :] == jnp.arange(cap, dtype=F32)[None, None, :, None])
        & (hot_mine[:, :, None, :] > 0.5)
    ).astype(BF)

    def dispatch(x):
        rows = jnp.einsum("esct,std->escd", place, x, preferred_element_type=F32).astype(BF)
        return lax.all_to_all(rows, "expert", split_axis=0, concat_axis=0, tiled=True).reshape(
            E * Z * cap, x.shape[-1]
        )

    def gates_of(logits, hot_in):
        chosen = jnp.where(hot_in > 0.5, logits, masked_score)
        top = jnp.max(chosen, -1, keepdims=True)
        parts_in = jnp.where(hot_in > 0.5, jnp.exp(chosen - top), 0.0)
        return parts_in / jnp.maximum(jnp.sum(parts_in, -1, keepdims=True), 0.5)

    grad_rows_hot = dispatch(grad_hot)

    inner_z = gather_z(after(inner, grad_hot, up_far))
    near = fetch(1, 0, 2, inner_z)
    front = [[piece_of(0, 0, 1), near[:1], gate_far], [piece_of(0, 1, 2), near[1:], up_far]]
    last = up_far
    for k in range(3, Z):
        for m in range(2):
            last = fetch(k, m, m + 1, last)
            front[m].append(last)
    rows = dispatch(after(inner_z, grad_rows_hot, *[f[3] for f in front[:1] if Z > 3]))
    down = [piece_of(0, 2, 3)] + [fetch(k, 2, 3, last) for k in range(1, Z)]

    place_of = jnp.stack([zi, ei * local + first]).astype(jnp.int32)
    router_wide = packed[:, D:]
    eg, eu, gated, gate_col = expert_front(place_of, rows, grad_rows_hot, router_wide, front[0] + front[1])
    down_grad = weight_grads(grad_rows_hot, [gated], D)

    def send_grads(g, last):
        got = [None] * Z
        for k in [0] + list(range(2, Z)):
            piece = lax.dynamic_slice(g, (0, (zi ^ k) * deep, 0), (g.shape[0], deep, FP))
            if k > 0:
                piece = after(piece, last) if last is not None else piece
                piece = lax.ppermute(piece, "dp", [(i, i ^ k) for i in range(Z)])
                last = piece
            got[k] = piece
        return got, last

    def send_near(g, *needed):
        piece = lax.dynamic_slice(g, (0, (zi ^ 1) * deep, 0), (g.shape[0], deep, FP))
        return lax.ppermute(after(piece, *needed), "dp", [(i, i ^ 1) for i in range(Z)])

    down_got, last_down = send_grads(down_grad, None)
    rows_grad, routed_rows, eg_grad, eu_grad, gate_grad = expert_back(
        place_of, grad_rows_hot, eg, eu, after(gated, down_grad), gate_col, front[0] + front[1], down,
        Z * cap,
    )

    gate_grad_back = lax.all_to_all(
        gate_grad, "expert", split_axis=0, concat_axis=0, tiled=True
    )[:, 0].reshape(E, Z, cap)
    front_grad = weight_grads(
        after(rows, gate_grad_back, down_got[2]), [eg_grad, eu_grad], D
    )
    front_got, _ = send_grads(front_grad, last_down)

    flat_inner = after(inner_z, front_grad).reshape(Z * L, D)
    flat_grad = grad_in.reshape(Z * L, D)
    sg = mm(flat_inner, shared_w[0])
    su = mm(flat_inner, shared_w[1])
    ssig = jax.nn.sigmoid(sg)
    ssilu = sg * ssig
    shared_hidden = (ssilu * su).astype(BF)
    shared_out = mm_nt(shared_hidden, shared_w[2])
    shared_hidden_grad = mm(flat_grad, shared_w[2])
    sg_grad = (shared_hidden_grad * su * ssig * (1.0 + sg * (1.0 - ssig))).astype(BF)
    su_grad = (shared_hidden_grad * ssilu).astype(BF)
    shared_back = mm_nt(sg_grad, shared_w[0]) + mm_nt(su_grad, shared_w[1])
    shared_grads = jnp.stack(
        [mm_tn(flat_inner, sg_grad), mm_tn(flat_inner, su_grad), mm_tn(flat_grad, shared_hidden)]
    ).astype(BF)

    def collect(rows_in, add):
        back = lax.all_to_all(
            rows_in.reshape(E, Z, cap, D), "expert", split_axis=0, concat_axis=0, tiled=True
        )
        total = jnp.einsum("esct,escd->std", place, back, preferred_element_type=F32) + add
        return back, total.astype(BF)

    gate_grad_mine = jnp.sum(place.astype(F32) * gate_grad_back[:, :, :, None], 2)
    gate_grad_z = jnp.einsum(
        "est,xe->stx", gate_grad_mine, pick, precision=lax.Precision.HIGHEST
    ).reshape(Z * L, experts)
    gates_z = gates_of(mm(flat_inner, router_w), hot.reshape(Z * L, experts))
    logit_grad = gates_z * (gate_grad_z - jnp.sum(gates_z * gate_grad_z, -1, keepdims=True))
    router_grad = mm_tn(flat_inner.astype(F32), logit_grad)
    router_back = mm_nt(logit_grad, router_w.astype(F32))

    rows_back, inner_grad = collect(rows_grad, (shared_back + router_back).reshape(Z, L, D))
    inner_grad = reduce_z(after(inner_grad, *down_got[2:]))
    routed_back, branch = collect(after(routed_rows, rows_back), shared_out.reshape(Z, L, D))

    def reduce_rows(x):
        x = jnp.swapaxes(x.reshape(Z, E, R, x.shape[1]), 0, 1).reshape(D, x.shape[1])
        x = lax.psum_scatter(x, "expert", scatter_dimension=0, tiled=True)
        x = x.reshape(Z, R, x.shape[1])
        return jnp.concatenate([lax.dynamic_slice_in_dim(x, zi ^ o, 1, 0) for o in offs], 0)

    middle_grad, attn_grad, second_gain_grad, proj_grad = attend_back(
        after(inner_grad, front_got[2]), cotangent, middle, packed, gain_row, heads_in, doc_row, doc_col, cosine, sine
    )
    output_grad = mm_tn(heads_out, attn_grad)
    pad = jnp.zeros((D, 128 - experts - 1), F32)
    small_all = jnp.concatenate(
        [output_grad, router_grad, second_gain_grad.T, pad], 1
    ).astype(BF)
    small_own = reduce_rows(small_all)

    proj_grad = lax.all_to_all(after(proj_grad, routed_back), "expert", split_axis=0, concat_axis=0, tiled=True)
    proj_grad = proj_grad.reshape(E * L, wide)
    proj_w_grad = mm_tn(unit_all, proj_grad).astype(BF).reshape(Z * E, R, wide)
    proj_w_local = proj_w_grad
    small_own = reduce_z(after(small_own, proj_w_local))
    proj_w_grad = lax.all_to_all(proj_w_grad, ALL, split_axis=0, concat_axis=0, tiled=True)
    proj_sum = jnp.sum(proj_w_grad.reshape(Z, E, R, wide).astype(F32), 0)
    proj_sum = jnp.swapaxes(proj_sum, 0, 1).reshape(R, E * wide)[:, : 3 * D]
    proj_sum = jnp.swapaxes(proj_sum.reshape(R, 3, D), 0, 1)

    back = mm_nt(proj_grad, w_proj).astype(BF)
    back_local = back
    scaled_first = lax.psum_scatter(back, "expert", scatter_dimension=0, tiled=True).astype(F32)
    input_grad = middle_grad + inv_first * (
        scaled_first - unit_first * jnp.mean(scaled_first * unit_first, -1, keepdims=True)
    )

    branch = reduce_z(after(branch, back_local, proj_w_local))
    layer_out = (middle + branch).astype(BF)
    first_mask = jnp.concatenate([jnp.ones((1,), bool), documents[1:] != documents[:-1]])
    kept_mask = 1.0 - first_mask.astype(F32)
    kept_total = jnp.sum(kept_mask) * D
    attn_rms = jnp.sqrt(jnp.sum(kept_mask * attn_square[:, 0]) / kept_total)
    branch_rms = jnp.sqrt(jnp.sum(kept_mask[:, None] * branch * branch) / kept_total)
    sublayer_rms = jnp.stack([attn_rms, branch_rms])[None, :]

    first_gain_grad = jnp.sum(proj_sum * attn_weight[:3].astype(BF).astype(F32), (0, 2))
    attn_sum = jnp.concatenate(
        [proj_sum * gain_low[0][None, :, None], small_own[None, :, :D]], 0
    )
    router_sum = small_own[:, D : D + experts]
    gain_sum = jnp.stack([first_gain_grad, small_own[:, D + experts]])

    owned = (expert_weight, expert_momentum, expert_average)
    expert_new = ()
    expert_sum = jnp.zeros((local, 3, deep, FF), BF)
    down_got[1] = send_near(down_grad, proj_w_local)
    front_got[1] = send_near(front_grad, proj_w_local)
    for k in [0] + list(range(2, Z)) + [1]:
        for m, gots in ((2, down_got), (0, front_got)):
            there = zi ^ k
            got = after(gots[k], proj_w_local, *((branch,) if m == 0 and k == 1 else ()))
            if parts == 1:
                expert_new = update_part(owned, expert_new, got, m, there)
            else:
                expert_sum = lax.dynamic_update_slice(
                    expert_sum, got[None], (there // parts, m, 0, (there % parts) * FP)
                )
    if parts > 1:
        expert_new = update(*owned, expert_sum.astype(F32), rate_expert)

    sgr = shared_grads.reshape(3, Z, E, R, FS).transpose(2, 1, 0, 3, 4).reshape(E * Z * 3 * R, FS)
    sgr = lax.psum_scatter(sgr, "expert", scatter_dimension=0, tiled=True)
    sgr = after(sgr.reshape(Z, 3, R, FS), proj_w_local)
    got = swap_z(
        [lax.dynamic_index_in_dim(sgr, zi ^ k, 0, keepdims=False) for k in range(Z)]
    )
    shared_sum = jnp.zeros((3, R, Z * FS), BF)
    for k in range(Z):
        shared_sum = lax.dynamic_update_slice(shared_sum, got[k], (0, 0, (zi ^ k) * FS))
    shared_sum = shared_sum.astype(F32)

    attn_rates = jnp.array([rate_attn, rate_attn, rate_attn, rate_output], F32).reshape(4, 1, 1)
    return (
        layer_out,
        input_grad,
        *update(attn_weight, attn_momentum, attn_average, attn_sum, attn_rates),
        *update(shared_weight, shared_momentum, shared_average, shared_sum, rate_shared),
        *update(router_weight, router_momentum, router_average, router_sum, rate_router),
        *update(gain_weight, gain_momentum, gain_average, gain_sum, rate_gain),
        *expert_new,
        sublayer_rms,
    )


def solution(mesh):
    rows = P(ALL, None)
    middle = P(None, ALL, None)
    gains = P(None, ALL)
    routed = P("expert", None, "dp", None)
    weights = (middle,) * 6 + (rows,) * 3 + (gains,) * 3 + (routed,) * 3
    return jax.shard_map(
        body,
        mesh=mesh,
        in_specs=(rows,) * 4 + weights,
        out_specs=(rows,) * 2 + weights + (rows,),
        check_vma=False,
    )
```

```python
import functools
import math

import jax
import jax.numpy as jnp
from jax import lax
from jax.experimental import pallas as pl
from jax.experimental.pallas import tpu as pltpu
from jax.sharding import PartitionSpec as P

HEADS = 10
HD = 128
TOPK = 7
STEP = 3
BF = jnp.bfloat16
F32 = jnp.float32

epsilon = 1e-06
momentum_decay = 0.9
masked_score = -1e30
rate_attn = 5e-05
rate_output = 0.0002
rate_shared = 0.0001
rate_router = 3e-05
rate_gain = 0.002
rate_expert = 0.0015
ALL = ("dp", "expert")


def rope_tables(length, size):
    half = size // 2
    freq = jnp.exp(jnp.arange(half, dtype=F32) * (-2.0 * math.log(10000.0) / size))
    angle = jnp.arange(length, dtype=F32)[:, None] * freq[None, :]
    cosine = jnp.concatenate([jnp.cos(angle), jnp.cos(angle)], -1)
    sine = jnp.concatenate([jnp.sin(angle), jnp.sin(angle)], -1)
    return (cosine, sine)


def update(weight, moment, average, grad, rate):
    moment_new = momentum_decay * moment + grad
    weight_new = weight - rate * (grad + momentum_decay * moment_new)
    average_new = average + (weight_new - average) / (STEP + 1.0)
    return (weight_new, moment_new, average_new)


def mm(a, b):
    return jnp.dot(a, b, preferred_element_type=F32)


def mm_nt(a, b):
    return lax.dot_general(a, b, (((1,), (1,)), ((), ())), preferred_element_type=F32)


def mm_tn(a, b):
    return lax.dot_general(a, b, (((0,), (0,)), ((), ())), preferred_element_type=F32)


def attend_probs(heads_ref, doc_row_ref, doc_col_ref, block):
    share = heads_ref.shape[2] // HD

    def head(b):
        return heads_ref[b // share, :, (b % share) * HD : (b % share + 1) * HD]

    length = heads_ref.shape[1]
    row = lax.broadcasted_iota(jnp.int32, (length, length), 0)
    col = lax.broadcasted_iota(jnp.int32, (length, length), 1)
    allowed = (col <= row) & (doc_row_ref[...] == doc_col_ref[...])
    query, key = head(block), head(HEADS + block)
    scores = jnp.where(allowed, mm_nt(query, key) * HD ** (-0.5), masked_score)
    exponent = jnp.exp(scores - jnp.max(scores, -1, keepdims=True))
    probs = exponent / jnp.sum(exponent, -1, keepdims=True)
    return query, key, head(2 * HEADS + block), probs


def attend_kernel(heads_ref, doc_row_ref, doc_col_ref, out_ref):
    for h in range(HEADS):
        _, _, value, probs = attend_probs(heads_ref, doc_row_ref, doc_col_ref, h)
        out_ref[:, h * HD : (h + 1) * HD] = mm(probs.astype(BF), value).astype(BF)


def attend(heads, doc_row, doc_col):
    return pl.pallas_call(
        attend_kernel,
        out_shape=jax.ShapeDtypeStruct((heads.shape[1], HEADS * HD), BF),
        compiler_params=pltpu.CompilerParams(vmem_limit_bytes=24 << 20),
        name="attend",
    )(heads, doc_row, doc_col)


def out_kernel(heads_ref, tokens_ref, w_ref, gain_ref, middle_ref, inner_ref, square_ref):
    attn_out = mm(heads_ref[...], w_ref[...])
    middle = tokens_ref[...].astype(F32) + attn_out
    scale = lax.rsqrt(jnp.mean(middle * middle, -1, keepdims=True) + epsilon)
    middle_ref[...] = middle
    inner_ref[...] = (middle * scale * gain_ref[...]).astype(BF)
    square = jnp.sum(attn_out * attn_out, -1, keepdims=True)
    square_ref[...] = jnp.broadcast_to(square, square_ref.shape)


def project_out(heads_out, tokens, packed, gain):
    length, width = tokens.shape
    return pl.pallas_call(
        out_kernel,
        grid=(1,),
        in_specs=[
            pl.BlockSpec((length, width), lambda i: (0, 0)),
            pl.BlockSpec((length, width), lambda i: (0, 0)),
            pl.BlockSpec((width, width), lambda i: (0, 0)),
            pl.BlockSpec((1, width), lambda i: (0, 0)),
        ],
        out_specs=[
            pl.BlockSpec((length, width), lambda i: (0, 0)),
            pl.BlockSpec((length, width), lambda i: (0, 0)),
            pl.BlockSpec((length, 128), lambda i: (0, 0)),
        ],
        out_shape=[
            jax.ShapeDtypeStruct((length, width), F32),
            jax.ShapeDtypeStruct((length, width), BF),
            jax.ShapeDtypeStruct((length, 128), F32),
        ],
        compiler_params=pltpu.CompilerParams(vmem_limit_bytes=24 << 20),
        name="project_out",
    )(heads_out, tokens, packed, gain)


def attend_back_kernel(
    ig_ref, g_ref, middle_ref, w_ref, gain_ref, heads_ref, doc_row_ref, doc_col_ref,
    cos_ref, sin_ref, mg_ref, ag_ref, gain_out, out_ref, hg_ref
):
    grad = ig_ref[...]
    middle = middle_ref[...]
    scale = lax.rsqrt(jnp.mean(middle * middle, -1, keepdims=True) + epsilon)
    unit = middle * scale
    scaled = grad * gain_ref[...]
    gain_out[...] = jnp.sum(grad * unit, 0, keepdims=True)
    middle_grad = g_ref[...].astype(F32) + scale * (
        scaled - unit * jnp.mean(scaled * unit, -1, keepdims=True)
    )
    mg_ref[...] = middle_grad
    attn_grad = middle_grad.astype(BF)
    ag_ref[...] = attn_grad
    hg_ref[...] = mm_nt(attn_grad, w_ref[...]).astype(BF)
    share = heads_ref.shape[2] // HD

    def put(b, value):
        out_ref[b // share, :, (b % share) * HD : (b % share + 1) * HD] = value

    lane = lax.broadcasted_iota(jnp.int32, cos_ref.shape, 1)
    sign_sin = jnp.where(lane < HD // 2, -sin_ref[...], sin_ref[...])

    def rotate_back(z):
        return (z * cos_ref[...] + pltpu.roll(z * sign_sin, HD // 2, 1)).astype(BF)

    for h in range(HEADS):
        query, key, value, probs = attend_probs(heads_ref, doc_row_ref, doc_col_ref, h)
        out_grad = hg_ref[:, h * HD : (h + 1) * HD]
        prob_grad = mm_nt(out_grad, value)
        score_grad = (
            probs * (prob_grad - jnp.sum(probs * prob_grad, -1, keepdims=True))
        ).astype(BF)
        put(h, rotate_back(mm(score_grad, key) * HD ** (-0.5)))
        put(HEADS + h, rotate_back(mm_tn(score_grad, query) * HD ** (-0.5)))
        put(2 * HEADS + h, mm_tn(probs.astype(BF), out_grad).astype(BF))
    for b in range(3 * HEADS, heads_ref.shape[0] * share):
        put(b, jnp.zeros((heads_ref.shape[1], HD), BF))


def attend_back(grad, cotangent, middle, packed, gain, heads, doc_row, doc_col, cosine, sine):
    length, width = middle.shape
    whole = pl.BlockSpec((length, width), lambda i: (0, 0))
    table = pl.BlockSpec((length, HD), lambda i: (0, 0))
    row = pl.BlockSpec((1, width), lambda i: (0, 0))
    blocks = pl.BlockSpec(heads.shape, lambda i: (0, 0, 0))
    return pl.pallas_call(
        attend_back_kernel,
        grid=(1,),
        in_specs=[
            whole,
            whole,
            whole,
            pl.BlockSpec((width, width), lambda i: (0, 0)),
            row,
            blocks,
            pl.BlockSpec((1, length), lambda i: (0, 0)),
            pl.BlockSpec((length, 1), lambda i: (0, 0)),
            table,
            table,
        ],
        out_specs=[whole, whole, row, blocks],
        out_shape=[
            jax.ShapeDtypeStruct((length, width), F32),
            jax.ShapeDtypeStruct((length, width), BF),
            jax.ShapeDtypeStruct((1, width), F32),
            jax.ShapeDtypeStruct(heads.shape, BF),
        ],
        scratch_shapes=[pltpu.VMEM((length, width), BF)],
        compiler_params=pltpu.CompilerParams(vmem_limit_bytes=32 << 20),
        name="attend_back",
    )(grad, cotangent, middle, packed, gain, heads, doc_row, doc_col, cosine, sine)


def load_pieces(zi, pieces, dest, sem):
    depth = pieces[0].shape[1]
    copies = [
        pltpu.make_async_copy(
            piece,
            dest.at[:, pl.ds(pl.multiple_of((zi ^ k) * depth, 16), depth)],
            sem.at[k],
        )
        for k, piece in enumerate(pieces)
    ]
    for copy in copies:
        copy.start()
    for copy in copies:
        copy.wait()


def front_kernel(count, place_ref, x_ref, hot_ref, router_ref, *rest):
    pieces = rest[:count]
    eg_ref, eu_ref, gated_ref, gate_ref, w_ref, sem = rest[count:]

    @pl.when(pl.program_id(0) == 0)
    def _():
        half = count // 2
        load_pieces(place_ref[0], pieces[:half], w_ref.at[pl.ds(0, 1)], sem)
        load_pieces(place_ref[0], pieces[half:], w_ref.at[pl.ds(1, 1)], sem)

    x = x_ref[...]
    hot = hot_ref[...].astype(F32) > 0.5
    chosen = jnp.where(hot, mm(x, router_ref[...]), masked_score)
    top = jnp.max(chosen, -1, keepdims=True)
    exponent = jnp.where(hot, jnp.exp(chosen - top), 0.0)
    lane = lax.broadcasted_iota(jnp.int32, exponent.shape, 1)
    own = jnp.sum(jnp.where(lane == place_ref[1], exponent, 0.0), -1, keepdims=True)
    gate = own / jnp.maximum(jnp.sum(exponent, -1, keepdims=True), 0.5)
    eg = mm(x, w_ref[0])
    eu = mm(x, w_ref[1])
    eg_ref[...] = eg
    eu_ref[...] = eu
    gated_ref[...] = (gate * (eg * jax.nn.sigmoid(eg) * eu)).astype(BF)
    gate_ref[...] = jnp.broadcast_to(gate, gate_ref.shape)


def tile_of(count):
    return next(t for t in (256, 192, 128, 64, 48, 16, 8) if count % t == 0)


def expert_front(place, rows, grads_hot, router, pieces):
    count, width = rows.shape
    hidden = pieces[0].shape[2]
    tile = tile_of(count)
    extra = grads_hot.shape[1] - width
    flops = 4 * count * width * hidden
    return pl.pallas_call(
        functools.partial(front_kernel, len(pieces)),
        grid_spec=pltpu.PrefetchScalarGridSpec(
            num_scalar_prefetch=1,
            grid=(count // tile,),
            in_specs=[
                pl.BlockSpec((tile, width), lambda i, p: (i, 0)),
                pl.BlockSpec((tile, extra), lambda i, p: (i, width // extra)),
                pl.BlockSpec((width, extra), lambda i, p: (0, 0)),
            ]
            + [pl.BlockSpec(memory_space=pl.ANY)] * len(pieces),
            out_specs=[pl.BlockSpec((tile, hidden), lambda i, p: (i, 0))] * 3
            + [pl.BlockSpec((tile, 128), lambda i, p: (i, 0))],
            scratch_shapes=[
                pltpu.VMEM((2, width, hidden), BF),
                pltpu.SemaphoreType.DMA((len(pieces),)),
            ],
        ),
        out_shape=[
            jax.ShapeDtypeStruct((count, hidden), F32),
            jax.ShapeDtypeStruct((count, hidden), F32),
            jax.ShapeDtypeStruct((count, hidden), BF),
            jax.ShapeDtypeStruct((count, 128), F32),
        ],
        cost_estimate=pl.CostEstimate(
            flops=flops, bytes_accessed=12 * count * hidden, transcendentals=0
        ),
        compiler_params=pltpu.CompilerParams(vmem_limit_bytes=40 << 20),
        name="expert_front",
    )(place, rows, grads_hot, router, *pieces)


def back_kernel(count, place_ref, g_ref, eg_ref, eu_ref, gated_ref, gate_ref, *rest):
    gate_w, up_w, down = rest[:count], rest[count : 2 * count], rest[2 * count : 3 * count]
    rows_ref, routed_ref, egg_ref, eug_ref, gg_ref, w_ref, wd_ref, sem = rest[3 * count :]

    @pl.when(pl.program_id(0) == 0)
    def _():
        load_pieces(place_ref[0], down, wd_ref, sem)
        load_pieces(place_ref[0], gate_w, w_ref.at[pl.ds(0, 1)], sem)
        load_pieces(place_ref[0], up_w, w_ref.at[pl.ds(1, 1)], sem)

    eg = eg_ref[...]
    eu = eu_ref[...]
    sig = jax.nn.sigmoid(eg)
    silu = eg * sig
    plain = mm(g_ref[...], wd_ref[0])
    gate_grad = jnp.sum(silu * eu * plain, -1, keepdims=True)
    count = gg_ref.shape[2]
    for i in range(gg_ref.shape[0]):
        part = gate_grad[i * count : (i + 1) * count]
        gg_ref[i] = jnp.broadcast_to(part, (count, 128)).T[:8]
    grad = gate_ref[:, :1] * plain
    eg_grad = (grad * eu * sig * (1.0 + eg * (1.0 - sig))).astype(BF)
    eu_grad = (grad * silu).astype(BF)
    egg_ref[...] = eg_grad
    eug_ref[...] = eu_grad
    rows_ref[...] = (mm_nt(eg_grad, w_ref[0]) + mm_nt(eu_grad, w_ref[1])).astype(BF)
    routed_ref[...] = mm_nt(gated_ref[...], wd_ref[0]).astype(BF)


def expert_back(place, grads_hot, eg, eu, gated, gate, front, down, group):
    count, hidden = eg.shape
    deep = front[0].shape[1]
    width = deep * len(down)
    tile = 2 * group if count % (2 * group) == 0 else group
    wide = pl.BlockSpec((tile, width), lambda i, p: (i, 0))
    thin = pl.BlockSpec((tile, hidden), lambda i, p: (i, 0))
    lanes = pl.BlockSpec((tile, 128), lambda i, p: (i, 0))
    return pl.pallas_call(
        functools.partial(back_kernel, len(down)),
        grid_spec=pltpu.PrefetchScalarGridSpec(
            num_scalar_prefetch=1,
            grid=(count // tile,),
            in_specs=[wide, thin, thin, thin, lanes]
            + [pl.BlockSpec(memory_space=pl.ANY)] * (3 * len(down)),
            out_specs=[wide, wide, thin, thin, pl.BlockSpec((tile // group, 8, group), lambda i, p: (i, 0, 0))],
            scratch_shapes=[
                pltpu.VMEM((2, width, hidden), BF),
                pltpu.VMEM((1, width, hidden), BF),
                pltpu.SemaphoreType.DMA((len(down),)),
            ],
        ),
        out_shape=[
            jax.ShapeDtypeStruct((count, width), BF),
            jax.ShapeDtypeStruct((count, width), BF),
            jax.ShapeDtypeStruct((count, hidden), BF),
            jax.ShapeDtypeStruct((count, hidden), BF),
            jax.ShapeDtypeStruct((count // group, 8, group), F32),
        ],
        cost_estimate=pl.CostEstimate(
            flops=8 * count * width * hidden,
            bytes_accessed=16 * count * hidden,
            transcendentals=0,
        ),
        compiler_params=pltpu.CompilerParams(vmem_limit_bytes=48 << 20),
        name="expert_back",
    )(place, grads_hot, eg, eu, gated, gate, *front, *down)


def weight_grads(x, ys, width):
    count = x.shape[0]
    hidden = ys[0].shape[1]
    tile = 256
    return pl.pallas_call(
        grads_body(len(ys)),
        grid=(width // tile,),
        in_specs=[pl.BlockSpec((count, tile), lambda i: (0, i))]
        + [pl.BlockSpec((count, hidden), lambda i: (0, 0))] * len(ys),
        out_specs=pl.BlockSpec((len(ys), tile, hidden), lambda i: (0, i, 0)),
        out_shape=jax.ShapeDtypeStruct((len(ys), width, hidden), BF),
        cost_estimate=pl.CostEstimate(
            flops=2 * len(ys) * count * width * hidden,
            bytes_accessed=2 * count * (width + hidden),
            transcendentals=0,
        ),
        compiler_params=pltpu.CompilerParams(vmem_limit_bytes=40 << 20),
        name="weight_grads",
    )(x, *ys)


def grads_body(many):
    def kernel(x_ref, *rest):
        x = x_ref[...]
        for i in range(many):
            rest[many][i] = mm_tn(x, rest[i][...]).astype(BF)

    return kernel


def update_kernel(place_ref, w_ref, m_ref, a_ref, g_ref, *rest):
    w_out, m_out, a_out = rest[-3:]
    new = update(w_ref[0, 0], m_ref[0, 0], a_ref[0, 0], g_ref[0].astype(F32), rate_expert)
    w_out[0, 0], m_out[0, 0], a_out[0, 0] = new


def update_part(owned, so_far, grad, low, place):
    count, deep, width = grad.shape
    tile = deep // 2
    state = pl.BlockSpec((1, 1, tile, width), lambda m, t, p: (p[0], low + m, t, 0))
    moved = 6 * 4 * grad.size + 2 * grad.size
    return pl.pallas_call(
        update_kernel,
        grid_spec=pltpu.PrefetchScalarGridSpec(
            num_scalar_prefetch=1,
            grid=(count, deep // tile),
            in_specs=[state] * 3
            + [pl.BlockSpec((1, tile, width), lambda m, t, p: (m, t, 0))]
            + [pl.BlockSpec(memory_space=pl.ANY)] * len(so_far),
            out_specs=[state] * 3,
        ),
        out_shape=[jax.ShapeDtypeStruct(x.shape, x.dtype) for x in owned],
        input_output_aliases={5 + i: i for i in range(len(so_far))},
        cost_estimate=pl.CostEstimate(
            flops=8 * grad.size, bytes_accessed=moved, transcendentals=0
        ),
        compiler_params=pltpu.CompilerParams(vmem_limit_bytes=60 << 20),
        name="update_part",
    )(jnp.reshape(place, (1,)).astype(jnp.int32), *owned, grad, *so_far)


def body(
    tokens,
    cotangent,
    routes,
    doc_ids,
    attn_weight,
    attn_momentum,
    attn_average,
    shared_weight,
    shared_momentum,
    shared_average,
    router_weight,
    router_momentum,
    router_average,
    gain_weight,
    gain_momentum,
    gain_average,
    expert_weight,
    expert_momentum,
    expert_average,
):
    Z = lax.axis_size("dp")
    E = lax.axis_size("expert")
    L, D = tokens.shape
    rows_own = attn_weight.shape[1]
    local, _, deep, FF = expert_weight.shape
    experts = router_weight.shape[1]
    parts = Z // local
    FP = FF // parts
    FS = shared_weight.shape[2] // Z
    cap = min(L, (L * TOPK * 3 // (2 * experts) + 7) // 8 * 8)
    zi = lax.axis_index("dp")

    def swap_z(pieces):
        out = [pieces[0]]
        for k in range(1, Z):
            out.append(lax.ppermute(pieces[k], "dp", [(i, i ^ k) for i in range(Z)]))
        return out

    strides = [1 << b for b in range(Z.bit_length() - 1)][::-1]
    offs = [0]
    for stride in strides:
        offs = offs + [o ^ stride for o in offs]

    def gather_z(x, then=()):
        held = x[None]
        for step, stride in enumerate(strides):
            if step > 0 and then:
                held = after(held, *then)
            got = lax.ppermute(held, "dp", [(i, i ^ stride) for i in range(Z)])
            held = jnp.concatenate([held, got], 0)
        return held

    def reduce_z(x):
        for stride in strides[::-1]:
            keep, send = jnp.split(x, 2, 0)
            got = lax.ppermute(send, "dp", [(i, i ^ stride) for i in range(Z)])
            total = keep.astype(F32) + got.astype(F32)
            x = total.astype(BF)
        return total[0]

    R = rows_own
    ei = lax.axis_index("expert")

    def after(x, *needed):
        return lax.optimization_barrier((x,) + needed)[0]

    blocks = 3 * D // HD
    share = -(-blocks // E)
    wide = share * HD
    gain_low = gain_weight.astype(BF).astype(F32)
    folded = (attn_weight[:3].astype(BF).astype(F32) * gain_low[0][None, :, None]).astype(BF)
    folded = jnp.swapaxes(folded, 0, 1).reshape(R, 3 * D)
    folded = jnp.pad(folded, ((0, 0), (0, E * wide - 3 * D)))
    folded = jnp.swapaxes(folded.reshape(R, E, wide), 0, 1)
    folded = jnp.broadcast_to(folded[None], (Z, E, R, wide)).reshape(Z * E, R, wide)
    w_proj = lax.all_to_all(folded, ALL, split_axis=0, concat_axis=0, tiled=True)
    w_proj = w_proj.reshape(D, wide)

    inputs = tokens.astype(F32)
    inv_first = lax.rsqrt(jnp.mean(inputs * inputs, -1, keepdims=True) + epsilon)
    unit_first = inputs * inv_first
    unit_all = lax.all_gather(unit_first.astype(BF), "expert", axis=0, tiled=True)

    extra = jnp.concatenate([router_weight, gain_weight[1:].T], 1).astype(BF)
    extra = jnp.pad(extra, ((0, 0), (0, 128 - extra.shape[1])))
    packed = jnp.concatenate([attn_weight[3].astype(BF), extra], 1)
    packed = lax.all_gather(gather_z(packed), "expert", axis=0, tiled=False)
    full = jnp.zeros((Z, E, R, D + 128), BF)
    for k, o in enumerate(offs):
        full = lax.dynamic_update_slice(full, packed[:, k][None], (zi ^ o, 0, 0, 0))
    packed = full.reshape(D, D + 128)
    w_o = packed[:, :D]
    router_w = packed[:, D : D + experts]
    gain_second = packed[:, D + experts].astype(F32)

    def piece_of(k, low, high):
        there = zi ^ k
        w = lax.dynamic_slice(
            expert_weight,
            (there // parts, low, 0, (there % parts) * FP),
            (1, high - low, deep, FP),
        )
        return w[0].astype(BF)

    def fetch(k, low, high, *needed):
        return lax.ppermute(
            after(piece_of(k, low, high), *needed), "dp", [(i, i ^ k) for i in range(Z)]
        )

    gate_far = fetch(2, 0, 1, w_proj)
    up_far = fetch(2, 1, 2, gate_far)

    cosine, sine = rope_tables(L, HD)
    score_scale = HD ** (-0.5)
    documents = doc_ids[0]
    position = jnp.arange(L)
    allowed = (
        (position[None, :] <= position[:, None]) & (documents[None, :] == documents[:, None])
    )[None]
    turned = (lax.axis_index("expert") * share + jnp.arange(share)) < 2 * D // HD
    turned = turned[None, None, :, None].astype(F32)
    cos_mine = cosine[None, :, None, :] * turned + (1.0 - turned)
    sin_mine = sine[None, :, None, :] * turned
    projected = mm(unit_all, w_proj).reshape(E, L, share, HD)
    half = HD // 2
    crossed = jnp.concatenate([-projected[..., half:], projected[..., :half]], -1)
    heads_in = (projected * cos_mine + crossed * sin_mine).astype(BF).reshape(E, L, wide)
    hot_own = jnp.sum(
        (routes[:, :, None] == jnp.arange(experts, dtype=jnp.int32)).astype(F32), 1
    )
    hot_wide = jnp.pad(hot_own, ((0, 0), (0, 128 - experts))).astype(BF)
    grad_hot = jnp.concatenate([cotangent, hot_wide], 1)
    heads_in = lax.all_to_all(heads_in, "expert", split_axis=0, concat_axis=0, tiled=True)
    grad_hot = gather_z(after(grad_hot, w_proj), (heads_in,))
    grad_in = grad_hot[:, :, :D]
    hot = grad_hot[:, :, D : D + experts].astype(F32)

    doc_row = doc_ids.astype(jnp.int32)
    doc_col = doc_row.reshape(L, 1)
    heads_out = attend(after(heads_in, gate_far), doc_row, doc_col)
    gain_row = gain_second[None, :]
    middle, inner, attn_square = project_out(
        heads_out, tokens, packed, gain_row
    )

    sw = after(shared_weight, inner).astype(BF)
    sw = [lax.dynamic_slice(sw, (0, 0, (zi ^ k) * FS), (3, R, FS)) for k in range(Z)]
    sw = jnp.stack(swap_z(sw), 1)
    sw = lax.all_gather(sw, "expert", axis=2, tiled=False)
    full = jnp.zeros((3, Z, E, R, FS), BF)
    for k in range(Z):
        full = lax.dynamic_update_slice(full, sw[:, k][:, None], (0, zi ^ k, 0, 0, 0))
    shared_w = full.reshape(3, D, FS)

    before = (position[None, :] < position[:, None]).astype(BF)
    rank = jnp.einsum("tu,sux->stx", before, hot.astype(BF), preferred_element_type=F32)
    first = zi // parts
    mine = jnp.arange(E) * local + first
    pick = (jnp.arange(experts)[:, None] == mine[None, :]).astype(F32)
    hot_mine = jnp.einsum("stx,xe->est", hot, pick)
    rank_mine = jnp.einsum("stx,xe->est", rank, pick, precision=lax.Precision.HIGHEST)
    place = (
        (rank_mine[:, :, None, :] == jnp.arange(cap, dtype=F32)[None, None, :, None])
        & (hot_mine[:, :, None, :] > 0.5)
    ).astype(BF)

    def dispatch(x):
        rows = jnp.einsum("esct,std->escd", place, x, preferred_element_type=F32).astype(BF)
        return lax.all_to_all(rows, "expert", split_axis=0, concat_axis=0, tiled=True).reshape(
            E * Z * cap, x.shape[-1]
        )

    def gates_of(logits, hot_in):
        chosen = jnp.where(hot_in > 0.5, logits, masked_score)
        top = jnp.max(chosen, -1, keepdims=True)
        parts_in = jnp.where(hot_in > 0.5, jnp.exp(chosen - top), 0.0)
        return parts_in / jnp.maximum(jnp.sum(parts_in, -1, keepdims=True), 0.5)

    grad_rows_hot = dispatch(grad_hot)

    inner_z = gather_z(after(inner, grad_hot, up_far))
    near = fetch(1, 0, 2, inner_z)
    front = [[piece_of(0, 0, 1), near[:1], gate_far], [piece_of(0, 1, 2), near[1:], up_far]]
    last = up_far
    for k in range(3, Z):
        for m in range(2):
            last = fetch(k, m, m + 1, last)
            front[m].append(last)
    rows = dispatch(after(inner_z, grad_rows_hot, *[f[3] for f in front[:1] if Z > 3]))
    down = [piece_of(0, 2, 3)] + [fetch(k, 2, 3, last) for k in range(1, Z)]

    place_of = jnp.stack([zi, ei * local + first]).astype(jnp.int32)
    router_wide = packed[:, D:]
    eg, eu, gated, gate_col = expert_front(place_of, rows, grad_rows_hot, router_wide, front[0] + front[1])
    down_grad = weight_grads(grad_rows_hot, [gated], D)

    def send_grads(g, last):
        got = [None] * Z
        for k in [0] + list(range(2, Z)):
            piece = lax.dynamic_slice(g, (0, (zi ^ k) * deep, 0), (g.shape[0], deep, FP))
            if k > 0:
                piece = after(piece, last) if last is not None else piece
                piece = lax.ppermute(piece, "dp", [(i, i ^ k) for i in range(Z)])
                last = piece
            got[k] = piece
        return got, last

    def send_near(g, *needed):
        piece = lax.dynamic_slice(g, (0, (zi ^ 1) * deep, 0), (g.shape[0], deep, FP))
        return lax.ppermute(after(piece, *needed), "dp", [(i, i ^ 1) for i in range(Z)])

    down_got, last_down = send_grads(down_grad, None)
    rows_grad, routed_rows, eg_grad, eu_grad, gate_grad = expert_back(
        place_of, grad_rows_hot, eg, eu, after(gated, down_grad), gate_col, front[0] + front[1], down,
        Z * cap,
    )

    gate_grad_back = lax.all_to_all(
        gate_grad, "expert", split_axis=0, concat_axis=0, tiled=True
    )[:, 0].reshape(E, Z, cap)
    front_grad = weight_grads(
        after(rows, gate_grad_back, down_got[2]), [eg_grad, eu_grad], D
    )
    front_got, _ = send_grads(front_grad, last_down)

    flat_inner = after(inner_z, front_grad).reshape(Z * L, D)
    flat_grad = grad_in.reshape(Z * L, D)
    sg = mm(flat_inner, shared_w[0])
    su = mm(flat_inner, shared_w[1])
    ssig = jax.nn.sigmoid(sg)
    ssilu = sg * ssig
    shared_hidden = (ssilu * su).astype(BF)
    shared_out = mm_nt(shared_hidden, shared_w[2])
    shared_hidden_grad = mm(flat_grad, shared_w[2])
    sg_grad = (shared_hidden_grad * su * ssig * (1.0 + sg * (1.0 - ssig))).astype(BF)
    su_grad = (shared_hidden_grad * ssilu).astype(BF)
    shared_back = mm_nt(sg_grad, shared_w[0]) + mm_nt(su_grad, shared_w[1])
    shared_grads = jnp.stack(
        [mm_tn(flat_inner, sg_grad), mm_tn(flat_inner, su_grad), mm_tn(flat_grad, shared_hidden)]
    ).astype(BF)

    def collect(rows_in, add):
        back = lax.all_to_all(
            rows_in.reshape(E, Z, cap, D), "expert", split_axis=0, concat_axis=0, tiled=True
        )
        total = jnp.einsum("esct,escd->std", place, back, preferred_element_type=F32) + add
        return back, total.astype(BF)

    gate_grad_mine = jnp.sum(place.astype(F32) * gate_grad_back[:, :, :, None], 2)
    gate_grad_z = jnp.einsum(
        "est,xe->stx", gate_grad_mine, pick, precision=lax.Precision.HIGHEST
    ).reshape(Z * L, experts)
    gates_z = gates_of(mm(flat_inner, router_w), hot.reshape(Z * L, experts))
    logit_grad = gates_z * (gate_grad_z - jnp.sum(gates_z * gate_grad_z, -1, keepdims=True))
    router_grad = mm_tn(flat_inner.astype(F32), logit_grad)
    router_back = mm_nt(logit_grad, router_w.astype(F32))

    rows_back, inner_grad = collect(rows_grad, (shared_back + router_back).reshape(Z, L, D))
    inner_grad = reduce_z(after(inner_grad, *down_got[2:]))
    routed_back, branch = collect(after(routed_rows, rows_back), shared_out.reshape(Z, L, D))

    def reduce_rows(x):
        x = jnp.swapaxes(x.reshape(Z, E, R, x.shape[1]), 0, 1).reshape(D, x.shape[1])
        x = lax.psum_scatter(x, "expert", scatter_dimension=0, tiled=True)
        x = x.reshape(Z, R, x.shape[1])
        return jnp.concatenate([lax.dynamic_slice_in_dim(x, zi ^ o, 1, 0) for o in offs], 0)

    middle_grad, attn_grad, second_gain_grad, proj_grad = attend_back(
        after(inner_grad, routed_back, front_got[2]), cotangent, middle, packed, gain_row, heads_in, doc_row, doc_col, cosine, sine
    )
    output_grad = mm_tn(heads_out, attn_grad)
    pad = jnp.zeros((D, 128 - experts - 1), F32)
    small_all = jnp.concatenate(
        [output_grad, router_grad, second_gain_grad.T, pad], 1
    ).astype(BF)
    small_own = reduce_rows(small_all)

    proj_grad = lax.all_to_all(after(proj_grad, small_all), "expert", split_axis=0, concat_axis=0, tiled=True)
    proj_grad = proj_grad.reshape(E * L, wide)
    proj_w_grad = mm_tn(unit_all, proj_grad).astype(BF).reshape(Z * E, R, wide)
    proj_w_local = proj_w_grad
    small_own = reduce_z(after(small_own, proj_w_local))
    proj_w_grad = lax.all_to_all(proj_w_grad, ALL, split_axis=0, concat_axis=0, tiled=True)
    proj_sum = jnp.sum(proj_w_grad.reshape(Z, E, R, wide).astype(F32), 0)
    proj_sum = jnp.swapaxes(proj_sum, 0, 1).reshape(R, E * wide)[:, : 3 * D]
    proj_sum = jnp.swapaxes(proj_sum.reshape(R, 3, D), 0, 1)

    back = mm_nt(proj_grad, w_proj).astype(BF)
    back_local = back
    scaled_first = lax.psum_scatter(back, "expert", scatter_dimension=0, tiled=True).astype(F32)
    input_grad = middle_grad + inv_first * (
        scaled_first - unit_first * jnp.mean(scaled_first * unit_first, -1, keepdims=True)
    )

    branch = reduce_z(after(branch, back_local, proj_w_local))
    layer_out = (middle + branch).astype(BF)
    first_mask = jnp.concatenate([jnp.ones((1,), bool), documents[1:] != documents[:-1]])
    kept_mask = 1.0 - first_mask.astype(F32)
    kept_total = jnp.sum(kept_mask) * D
    attn_rms = jnp.sqrt(jnp.sum(kept_mask * attn_square[:, 0]) / kept_total)
    branch_rms = jnp.sqrt(jnp.sum(kept_mask[:, None] * branch * branch) / kept_total)
    sublayer_rms = jnp.stack([attn_rms, branch_rms])[None, :]

    first_gain_grad = jnp.sum(proj_sum * attn_weight[:3].astype(BF).astype(F32), (0, 2))
    attn_sum = jnp.concatenate(
        [proj_sum * gain_low[0][None, :, None], small_own[None, :, :D]], 0
    )
    router_sum = small_own[:, D : D + experts]
    gain_sum = jnp.stack([first_gain_grad, small_own[:, D + experts]])

    owned = (expert_weight, expert_momentum, expert_average)
    expert_new = ()
    expert_sum = jnp.zeros((local, 3, deep, FF), BF)
    down_got[1] = send_near(down_grad, proj_w_local, proj_w_grad)
    front_got[1] = send_near(front_grad, proj_w_local)
    for k in [0] + list(range(2, Z)) + [1]:
        for m, gots in ((2, down_got), (0, front_got)):
            there = zi ^ k
            got = after(gots[k], proj_w_local, *((branch,) if m == 0 and k == 1 else ()))
            if parts == 1:
                expert_new = update_part(owned, expert_new, got, m, there)
            else:
                expert_sum = lax.dynamic_update_slice(
                    expert_sum, got[None], (there // parts, m, 0, (there % parts) * FP)
                )
    if parts > 1:
        expert_new = update(*owned, expert_sum.astype(F32), rate_expert)

    sgr = shared_grads.reshape(3, Z, E, R, FS).transpose(2, 1, 0, 3, 4).reshape(E * Z * 3 * R, FS)
    sgr = lax.psum_scatter(sgr, "expert", scatter_dimension=0, tiled=True)
    sgr = after(sgr.reshape(Z, 3, R, FS), proj_w_local)
    got = swap_z(
        [lax.dynamic_index_in_dim(sgr, zi ^ k, 0, keepdims=False) for k in range(Z)]
    )
    shared_sum = jnp.zeros((3, R, Z * FS), BF)
    for k in range(Z):
        shared_sum = lax.dynamic_update_slice(shared_sum, got[k], (0, 0, (zi ^ k) * FS))
    shared_sum = shared_sum.astype(F32)

    attn_rates = jnp.array([rate_attn, rate_attn, rate_attn, rate_output], F32).reshape(4, 1, 1)
    return (
        layer_out,
        input_grad,
        *update(attn_weight, attn_momentum, attn_average, attn_sum, attn_rates),
        *update(shared_weight, shared_momentum, shared_average, shared_sum, rate_shared),
        *update(router_weight, router_momentum, router_average, router_sum, rate_router),
        *update(gain_weight, gain_momentum, gain_average, gain_sum, rate_gain),
        *expert_new,
        sublayer_rms,
    )


def solution(mesh):
    rows = P(ALL, None)
    middle = P(None, ALL, None)
    gains = P(None, ALL)
    routed = P("expert", None, "dp", None)
    weights = (middle,) * 6 + (rows,) * 3 + (gains,) * 3 + (routed,) * 3
    return jax.shard_map(
        body,
        mesh=mesh,
        in_specs=(rows,) * 4 + weights,
        out_specs=(rows,) * 2 + weights + (rows,),
        check_vma=False,
    )
```
